512 devices in a mesh: ctx: 64 (over z, x, core), head: 8 (over y).
Axes of the slice: x: 4, y: 8, z: 8, core: 2. Of those that a mesh axis runs over, the one named last changes fastest.
Arguments:
- video_q: bfloat16 [4096, 3072], P('ctx', 'head'), may hold values from -51 to 51
- video_k: bfloat16 [4096, 3072], P('ctx', 'head'), may hold values from -4 to 4
- video_v: bfloat16 [4096, 3072], P('ctx', 'head'), may hold values from -6 to 6
- text_q: bfloat16 [256, 3072], P(None, 'head'), may hold values from -51 to 51
- text_k: bfloat16 [256, 3072], P(None, 'head'), may hold values from -4 to 4
- text_v: bfloat16 [256, 3072], P(None, 'head'), may hold values from -6 to 6
- tile_mask: int32 [32, 32], replicated, may hold values from 0 to 1, as said below
- out_weight: bfloat16 [3072, 3072], P('head'), may hold values from -0.109375 to 0.109375
Outputs:
- video_out: bfloat16 [4096, 3072], P('ctx', 'head')
- text_out: bfloat16 [256, 3072], P(None, 'head')
The draws below stay inside these ranges and needn't reach their ends.
Inputs may be any that keep to these rules, and one draw needn't show every extreme that they name: `tile_mask`: with tile t in frame t // 4 at position t % 4, entry [i, j] is 1 exactly when |position_i - position_j| * (1 + |frame_i - frame_j|) <= reach_i, for a reach_i of query tile i between 0 and 4; so every query tile reaches the tile at its own position in every frame.
All inputs are finite; a program needn't handle non-finite values.
Results may differ from the reference program's by a relative error of at most 0.029.
Values may be sent and summed in bfloat16 or wider, within the bound.
A program may use at most 192 MiB of HBM per device.

```python
import math
import jax
import jax.numpy as jnp
from jax import lax

D = 3072
HEADS = 24
HEAD_DIM = 128
TXT = 256
TILE = 128
TOKENS = 4096
TILES = 32
FRAME_TILES = 4


def query_draw(key, row_count):
    return jnp.clip(jax.random.normal(key, (row_count, D), jnp.float32), -4.0, 4.0)


def key_draw(key, row_count):
    return jnp.clip(jax.random.normal(key, (row_count, D), jnp.float32), -4.0, 4.0)


def draw_video_q(key, part):
    key = jax.random.fold_in(key, 3)
    return query_draw(key, TOKENS).astype(jnp.bfloat16)


def draw_video_k(key, part):
    key = jax.random.fold_in(key, 4)
    return key_draw(key, TOKENS).astype(jnp.bfloat16)


def draw_text_q(key, part):
    key = jax.random.fold_in(key, 5)
    return query_draw(key, TXT).astype(jnp.bfloat16)


def draw_text_k(key, part):
    key = jax.random.fold_in(key, 6)
    return key_draw(key, TXT).astype(jnp.bfloat16)


def draw_tile_mask(key, part):
    key = jax.random.fold_in(key, 11)
    reach = jax.random.randint(key, (TILES,), 0, FRAME_TILES + 1)
    tiles = jnp.arange(TILES)
    frame = tiles // FRAME_TILES
    position = tiles % FRAME_TILES
    distance = jnp.abs(frame[:, None] - frame[None, :])
    spacing = jnp.abs(position[:, None] - position[None, :])
    return (spacing * (1 + distance) <= reach[:, None]).astype(jnp.int32)


def shard_levels(key, dims, shards, smallest, top_value):
    level = 1.0
    for dim, shards_of in shards:
        draws = jax.random.uniform(jax.random.fold_in(jax.random.fold_in(key, 6), dim), (shards_of,), jnp.float32, smallest / len(shards), top_value / len(shards))
        level = level * jnp.repeat(jnp.exp(draws), dims[dim] // shards_of).reshape((-1,) + (1,) * (len(dims) - 1 - dim))
    return level


def normal_values(stream_key, extent, scale, most, pieces=(), held_as=jnp.bfloat16):
    array = scale * jax.random.normal(stream_key, extent, jnp.float32)
    if pieces:
        array = array * shard_levels(stream_key, extent, pieces, -0.22, 0.18)
    return jnp.clip(array, -most, most).astype(held_as)


def setup_inputs(seed: int = 0) -> dict:
    seeds = jax.random.split(jax.random.key(seed), 9)
    video_q = draw_video_q(jax.random.fold_in(seeds[8], 71), 0)
    video_k = draw_video_k(jax.random.fold_in(seeds[8], 71), 0)
    video_v = normal_values(seeds[2], (TOKENS, D), 1.0, 6.0, ((0, 64), (1, 8)))
    text_q = draw_text_q(jax.random.fold_in(seeds[8], 71), 0)
    text_k = draw_text_k(jax.random.fold_in(seeds[8], 71), 0)
    text_v = normal_values(seeds[5], (TXT, D), 1.0, 6.0, ((1, 8),))
    tile_mask = draw_tile_mask(jax.random.fold_in(seeds[8], 71), 0)
    out_weight = normal_values(seeds[7], (D, D), D ** -0.5, 0.109375, ((0, 8),))
    return dict(video_q=video_q, video_k=video_k, video_v=video_v, text_q=text_q, text_k=text_k, text_v=text_v, tile_mask=tile_mask, out_weight=out_weight)


def attend(queries, key_rows, value_rows, allowed):
    scores = jnp.dot(queries, key_rows.T, preferred_element_type=jnp.float32) * (1.0 / math.sqrt(HEAD_DIM))
    scores = jnp.where(allowed, scores, -1e+30)
    highest = lax.optimization_barrier(jnp.max(scores, axis=1, keepdims=True))
    unnormalized = jnp.exp(scores - highest)
    row_total = lax.optimization_barrier(jnp.sum(unnormalized, axis=1, keepdims=True))
    summed = jnp.dot(unnormalized.astype(jnp.bfloat16), value_rows, preferred_element_type=jnp.float32)
    return (summed / row_total).astype(jnp.bfloat16)

def reference(video_q, video_k, video_v, text_q, text_k, text_v, tile_mask, out_weight):
    all_keys = jnp.concatenate([video_k, text_k], axis=0)
    all_values = jnp.concatenate([video_v, text_v], axis=0)
    reached = jnp.repeat(jnp.repeat(tile_mask, TILE, axis=0), TILE, axis=1) > 0
    allowed = jnp.concatenate([reached, jnp.ones((TOKENS, TXT), dtype=bool)], axis=1)
    text_allowed = jnp.ones((TXT, TOKENS + TXT), dtype=bool)

    def per_head(head_index):
        offset = head_index.astype(jnp.int32) * HEAD_DIM

        def head_slice(matrix):
            return lax.dynamic_slice_in_dim(matrix, offset, HEAD_DIM, 1)
        video_part = attend(head_slice(video_q), head_slice(all_keys), head_slice(all_values), allowed)
        text_part = attend(head_slice(text_q), head_slice(all_keys), head_slice(all_values), text_allowed)
        return (video_part, text_part)
    video_heads, text_heads = lax.map(per_head, jnp.arange(HEADS))
    video_attn = jnp.transpose(video_heads, (1, 0, 2)).reshape(TOKENS, D)
    text_out = jnp.transpose(text_heads, (1, 0, 2)).reshape(TXT, D)
    video_out = jnp.dot(video_attn, out_weight, preferred_element_type=jnp.float32).astype(jnp.bfloat16)
    return (video_out, text_out)
```

```python
import functools
import math

import jax
import jax.numpy as jnp
from jax import lax
from jax.experimental import pallas as pl
from jax.experimental.pallas import tpu as pltpu
from jax.sharding import PartitionSpec as P

HEAD_DIM = 128
ROWS = 64
HEADS = 3
NZ, NX, NY = 8, 4, 8
FEATURES = HEADS * HEAD_DIM
TXT_ROWS = 16
TXT_KEYS = 64
VIDEO_Q = NX * ROWS
QUERIES = VIDEO_Q + TXT_ROWS
MERGE = ROWS + TXT_ROWS
PACK = MERGE + 16
STEP_KEYS = 256
NEG = -1e30
SCALE = math.log2(math.e) / math.sqrt(HEAD_DIM)
MESH = pl.DeviceIdType.MESH
BF16, F32 = jnp.bfloat16, jnp.float32


def body(vq, vk, vv, tq, tk, tv, mask, w, out, tout,
         q, kv, tkv, bias, acc, top, osend, orecv, attn, wbuf, ysend, yrecv,
         load_sem, w_sem, q_send, q_recv, z_send, z_recv, s_send, s_recv,
         o_send, o_recv, y_send, y_recv, t_send, t_recv):
    ctx, y = lax.axis_index("ctx"), lax.axis_index("head")
    core, x, z = ctx % 2, (ctx // 2) % NX, ctx // (2 * NX)
    row_id = 2 * z + core

    def device(zz, xx, cc, yy):
        return ((zz * NX + xx) * 2 + cc, yy)

    def text_device(k):
        other = (row_id + k) % (2 * NZ)
        return device(other // 2, x, other % 2, y)

    up = device((z + 1) % NZ, x, core, y)
    down = device((z + NZ - 1) % NZ, x, core, y)
    sibling = device(z, x, 1 - core, y)

    def x_device(k):
        return device(z, (x + k) % NX, core, y)

    def y_device(k):
        return (ctx, (y + k) % NY)

    loads = []

    def load(src, dst):
        copy = pltpu.make_async_copy(src, dst, load_sem.at[len(loads)])
        copy.start()
        loads.append(copy)

    for h in range(HEADS):
        cols = pl.ds(h * HEAD_DIM, HEAD_DIM)
        load(vk.at[:, cols], kv.at[h, 0, core, 0])
        load(vv.at[:, cols], kv.at[h, 0, core, 1])
    load(vq, q.at[pl.ds(x * ROWS, ROWS)])
    load(tq.at[pl.ds(row_id * TXT_ROWS, TXT_ROWS)], q.at[pl.ds(VIDEO_Q, TXT_ROWS)])
    load(tk.at[pl.ds(x * TXT_KEYS, TXT_KEYS)], tkv.at[0, pl.ds(0, TXT_KEYS)])
    load(tv.at[pl.ds(x * TXT_KEYS, TXT_KEYS)], tkv.at[1, pl.ds(0, TXT_KEYS)])
    w_loads = []
    for k in range(NY):
        copy = pltpu.make_async_copy(
            w.at[:, pl.ds(((y + k) % NY) * FEATURES, FEATURES)], wbuf.at[k], w_sem.at[k])
        copy.start()
        w_loads.append(copy)

    barrier = pltpu.get_barrier_semaphore()
    peers = [text_device(k) for k in range(1, 2 * NZ)]
    peers += [x_device(k) for k in range(1, NX)]
    peers += [y_device(k) for k in range(1, NY)]
    for peer in peers:
        pl.semaphore_signal(barrier, inc=1, device_id=peer, device_id_type=MESH)

    zeros = jnp.zeros((QUERIES, HEAD_DIM), F32)
    for s in range(5):
        for half in range(2):
            cols = slice(half * HEAD_DIM, (half + 1) * HEAD_DIM)
            if s in (0, 4) and half == 1:
                if s == 0:
                    lane = lax.broadcasted_iota(jnp.int32, (QUERIES, HEAD_DIM), 1)
                    bias[0, :, cols] = jnp.where(lane < TXT_KEYS, 0.0, NEG).astype(F32)
                continue
            tile_z = (z + NZ - s) % NZ if half == 0 else (z + s) % NZ
            for xx in range(NX):
                reach = mask[z * NX + xx, tile_z * NX + x].astype(F32)
                bias[s, xx * ROWS:(xx + 1) * ROWS, cols] = jnp.full(
                    (ROWS, HEAD_DIM), (1.0 - reach) * NEG, F32)
            bias[s, VIDEO_Q:, cols] = zeros[:TXT_ROWS]
    tkv[0, TXT_KEYS:] = jnp.zeros((HEAD_DIM - TXT_KEYS, FEATURES), BF16)
    tkv[1, TXT_KEYS:] = jnp.zeros((HEAD_DIM - TXT_KEYS, FEATURES), BF16)

    for copy in loads:
        copy.wait()
    pl.semaphore_wait(barrier, len(peers))

    sent = []

    def remote(src, dst, send, recv, to):
        return pltpu.make_async_remote_copy(
            src_ref=src, dst_ref=dst, send_sem=send, recv_sem=recv,
            device_id=to, device_id_type=MESH)

    def start(copy):
        copy.start()
        sent.append(copy)

    def z_copy(h, direction, d):
        here = d - 1 if direction == 0 else (NZ - d + 1) % NZ
        there = d if direction == 0 else NZ - d
        src, dst = kv.at[h, here, core], kv.at[h, there, core]
        if d == 4:
            src, dst = src.at[direction], dst.at[direction]
        return remote(src, dst, z_send.at[h, direction, d - 1], z_recv.at[h, direction, d - 1],
                      up if direction == 0 else down)

    def s_copy(h, slot, part=None, cc=None):
        cc = core if cc is None else cc
        ref = kv.at[h, slot, cc]
        index = slot
        if part is not None:
            ref, index = ref.at[part], slot if part == 0 else NZ
        return remote(ref, ref, s_send.at[h, index], s_recv.at[h, index], sibling)

    for h in range(HEADS):
        for direction in range(2):
            start(z_copy(h, direction, 1))
        start(s_copy(h, 0))

    q_ref = q.at[pl.ds(x * ROWS, ROWS)]
    for k in range(1, NX):
        start(remote(q_ref, q_ref, q_send.at[k], q_recv.at[k], x_device(k)))

    def wait_q():
        for k in range(1, NX):
            ref = q.at[pl.ds(((x + NX - k) % NX) * ROWS, ROWS)]
            remote(ref, ref, q_send.at[k], q_recv.at[k], x_device(k)).wait_recv()

    ones = jnp.ones((STEP_KEYS, HEAD_DIM), BF16)

    def absorb(h, s):
        cols = slice(h * HEAD_DIM, (h + 1) * HEAD_DIM)
        slots = {0: (0,), 4: (4,)}.get(s, (s, NZ - s))
        keys = [kv[h, slot, cc, 0] for slot in slots for cc in range(2)]
        values = [kv[h, slot, cc, 1] for slot in slots for cc in range(2)]
        if s == 0:
            keys.append(tkv[0, :, cols])
            values.append(tkv[1, :, cols])
        keys, values = jnp.concatenate(keys, 0), jnp.concatenate(values, 0)
        count = keys.shape[0]
        scores = lax.dot_general(q[:, cols], keys, (((1,), (1,)), ((), ())),
                                 preferred_element_type=F32)
        scores = scores * SCALE + bias[s, :, :count]
        high = jnp.max(scores, axis=1, keepdims=True)
        if s:
            before = top[h][:, :1]
            high = jnp.maximum(high, before)
        weights = jnp.exp2(scores - high).astype(BF16)
        values = jnp.concatenate([values, ones[:count]], 1)
        summed = jnp.dot(weights, values, preferred_element_type=F32)
        if s:
            summed = summed + acc[h] * jnp.exp2(before - high)
        acc[h] = summed
        top[h] = jnp.broadcast_to(high, (QUERIES, HEAD_DIM))

    def forward(h, d):
        for direction in range(2):
            z_copy(h, direction, d).wait_recv()
            if d < 4:
                start(z_copy(h, direction, d + 1))
                start(s_copy(h, d if direction == 0 else NZ - d))
            else:
                start(s_copy(h, 4, direction))

    def from_sibling(h, s):
        if s == 4:
            s_copy(h, 4, 0, 1 - core).wait_recv()
            s_copy(h, 4, 1, 1 - core).wait_recv()
        else:
            for slot in ((0,) if s == 0 else (s, NZ - s)):
                s_copy(h, slot, None, 1 - core).wait_recv()

    for h in range(HEADS):
        from_sibling(h, 0)
    wait_q()
    for d in range(1, 5):
        for h in range(HEADS):
            forward(h, d)
            if d > 1:
                from_sibling(h, d - 1)
            absorb(h, d - 1)

    eye = (lax.broadcasted_iota(jnp.int32, (MERGE, HEAD_DIM), 0)
           == lax.broadcasted_iota(jnp.int32, (MERGE, HEAD_DIM), 1))
    pad = jnp.zeros((13, HEAD_DIM), F32)

    def o_copy(h, k):
        return remote(osend.at[h, k], orecv.at[h, k], o_send.at[h, k], o_recv.at[h, k], x_device(k))

    for h in range(HEADS):
        from_sibling(h, 4)
        absorb(h, 4)
        total = acc[h, :, HEAD_DIM:]
        part = acc[h, :, :HEAD_DIM] / total
        acc[h, :, :HEAD_DIM] = part
        acc[h, :, HEAD_DIM:] = top[h] + jnp.log2(total)
        for k in (2, 1, 3, 0):
            to = pl.ds(pl.multiple_of(((x + k) % NX) * ROWS, ROWS), ROWS)
            block = jnp.concatenate([acc[h, to, :HEAD_DIM], acc[h, VIDEO_Q:, :HEAD_DIM]], 0)
            level = jnp.concatenate([acc[h, to, HEAD_DIM:], acc[h, VIDEO_Q:, HEAD_DIM:]], 0)
            row = jnp.sum(jnp.where(eye, level, 0.0), axis=0, keepdims=True)
            first = row.astype(BF16).astype(F32)
            second = (row - first).astype(BF16).astype(F32)
            third = row - first - second
            stats = jnp.concatenate([first, second, third, pad], 0)
            packed = jnp.concatenate([block, stats], 0).astype(BF16)
            if k == 0:
                orecv[h, 0] = packed
            else:
                osend[h, k] = packed
                start(o_copy(h, k))

    for h in range(HEADS):
        for k in range(1, NX):
            o_copy(h, k).wait_recv()
        levels = []
        for k in range(NX):
            stats = orecv[h, k, MERGE:].astype(F32)
            row = stats[0:1] + stats[1:2] + stats[2:3]
            levels.append(jnp.sum(jnp.where(eye, jnp.broadcast_to(row, eye.shape), 0.0),
                                  axis=1, keepdims=True))
        high = functools.reduce(jnp.maximum, levels)
        shares = [jnp.exp2(level - high) for level in levels]
        total = functools.reduce(jnp.add, shares)
        merged = functools.reduce(
            jnp.add, [orecv[h, k, :MERGE].astype(F32) * (shares[k] / total) for k in range(NX)])
        attn[:, h * HEAD_DIM:(h + 1) * HEAD_DIM] = merged.astype(BF16)

    mine = pl.ds(pl.multiple_of(row_id * TXT_ROWS, TXT_ROWS), TXT_ROWS)
    tout[mine] = attn[ROWS:]

    def y_copy(k):
        return remote(ysend.at[k], yrecv.at[k], y_send.at[k], y_recv.at[k], y_device(k))

    for copy in w_loads:
        copy.wait()
    for k in (4, 3, 5, 2, 6, 1, 7):
        ysend[k] = jnp.dot(attn[:ROWS], wbuf[k], preferred_element_type=F32).astype(BF16)
        start(y_copy(k))
    for k in range(1, 2 * NZ):
        start(remote(tout.at[mine], tout.at[mine], t_send.at[k], t_recv.at[k], text_device(k)))
    total = jnp.dot(attn[:ROWS], wbuf[0], preferred_element_type=F32)
    for k in (1, 7, 2, 6, 3, 5, 4):
        y_copy(k).wait_recv()
        total = total + yrecv[k].astype(F32)
    out[...] = total.astype(BF16)

    for k in range(1, 2 * NZ):
        other = (row_id + 2 * NZ - k) % (2 * NZ)
        ref = tout.at[pl.ds(pl.multiple_of(other * TXT_ROWS, TXT_ROWS), TXT_ROWS)]
        remote(ref, ref, t_send.at[k], t_recv.at[k], text_device(k)).wait_recv()
    for copy in sent:
        copy.wait_send()


def local(video_q, video_k, video_v, text_q, text_k, text_v, tile_mask, out_weight):
    anywhere = pl.BlockSpec(memory_space=pl.ANY)
    vmem = pl.BlockSpec(memory_space=pltpu.VMEM)
    dma = pltpu.SemaphoreType.DMA
    return pl.pallas_call(
        body,
        out_shape=(
            jax.ShapeDtypeStruct((ROWS, FEATURES), BF16),
            jax.ShapeDtypeStruct((2 * NZ * TXT_ROWS, FEATURES), BF16),
        ),
        in_specs=[anywhere] * 6 + [pl.BlockSpec(memory_space=pltpu.SMEM), anywhere],
        out_specs=(vmem, vmem),
        scratch_shapes=[
            pltpu.VMEM((QUERIES, FEATURES), BF16),
            pltpu.VMEM((HEADS, NZ, 2, 2, ROWS, HEAD_DIM), BF16),
            pltpu.VMEM((2, HEAD_DIM, FEATURES), BF16),
            pltpu.VMEM((5, QUERIES, STEP_KEYS), F32),
            pltpu.VMEM((HEADS, QUERIES, 2 * HEAD_DIM), F32),
            pltpu.VMEM((HEADS, QUERIES, HEAD_DIM), F32),
            pltpu.VMEM((HEADS, NX, PACK, HEAD_DIM), BF16),
            pltpu.VMEM((HEADS, NX, PACK, HEAD_DIM), BF16),
            pltpu.VMEM((MERGE, FEATURES), BF16),
            pltpu.VMEM((NY, FEATURES, FEATURES), BF16),
            pltpu.VMEM((NY, ROWS, FEATURES), BF16),
            pltpu.VMEM((NY, ROWS, FEATURES), BF16),
            dma((10,)),
            dma((NY,)),
            dma((NX,)), dma((NX,)),
            dma((HEADS, 2, 4)), dma((HEADS, 2, 4)),
            dma((HEADS, NZ + 1)), dma((HEADS, NZ + 1)),
            dma((HEADS, NX)), dma((HEADS, NX)),
            dma((NY,)), dma((NY,)),
            dma((2 * NZ,)), dma((2 * NZ,)),
        ],
        compiler_params=pltpu.CompilerParams(
            collective_id=0, has_side_effects=True, vmem_limit_bytes=40 * 2**20),
    )(video_q, video_k, video_v, text_q, text_k, text_v, tile_mask, out_weight)


def solution(mesh):
    placed = (
        P("ctx", "head"),
        P("ctx", "head"),
        P("ctx", "head"),
        P(None, "head"),
        P(None, "head"),
        P(None, "head"),
        P(),
        P("head", None),
    )
    return jax.shard_map(
        local,
        mesh=mesh,
        in_specs=placed,
        out_specs=(P("ctx", "head"), P(None, "head")),
        check_vma=False,
    )
```

```python
import functools
import math

import jax
import jax.numpy as jnp
from jax import lax
from jax.experimental import pallas as pl
from jax.experimental.pallas import tpu as pltpu
from jax.sharding import PartitionSpec as P

HEAD_DIM = 128
ROWS = 64
HEADS = 3
NZ, NX, NY = 8, 4, 8
FEATURES = HEADS * HEAD_DIM
TXT_ROWS = 16
TXT_KEYS = 64
TEXT = 64
GROUP = {0: 0, 1: 80, 3: 144, 2: 208}
QUERIES = 272
USED = (272, 272, 208, 208, 80)
STEP_KEYS = 256
NEG = -1e30
SCALE = math.log2(math.e) / math.sqrt(HEAD_DIM)
MESH = pl.DeviceIdType.MESH
BF16, F32 = jnp.bfloat16, jnp.float32


def body(vq, vk, vv, tq, tk, tv, mask, w, out, tout,
         q, kv, tkv, bias, acc, top, osend, orecv, tsend, trecv, attn, wbuf, ysend, yrecv, yterm,
         load_sem, w_sem, q_send, q_recv, z_send, z_recv, s_send, s_recv,
         o_send, o_recv, x_send, x_recv, y_send, y_recv, t_send, t_recv, up_sem, down_sem):
    ctx, y = lax.axis_index("ctx"), lax.axis_index("head")
    core, x, z = ctx % 2, (ctx // 2) % NX, ctx // (2 * NX)
    row_id = 2 * z + core

    def device(zz, xx, cc, yy):
        return ((zz * NX + xx) * 2 + cc, yy)

    def text_device(k):
        other = (row_id + k) % (2 * NZ)
        return device(other // 2, x, other % 2, y)

    up = device((z + 1) % NZ, x, core, y)
    down = device((z + NZ - 1) % NZ, x, core, y)
    sibling = device(z, x, 1 - core, y)

    def x_device(k):
        return device(z, (x + k) % NX, core, y)

    def y_device(k):
        return (ctx, (y + k) % NY)

    def signal(sem, to):
        pl.semaphore_signal(sem, inc=1, device_id=to, device_id_type=MESH)

    barrier = pltpu.get_barrier_semaphore()
    peers = [up, down, sibling] + [x_device(k) for k in range(1, NX)]
    peers += [y_device(1), y_device(NY - 1)]
    for peer in peers:
        signal(barrier, peer)

    loads = []

    def load(src, dst):
        copy = pltpu.make_async_copy(src, dst, load_sem.at[len(loads)])
        copy.start()
        loads.append(copy)

    for h in range(HEADS):
        for part, ref in enumerate((vk, vv)):
            load(ref.at[:, pl.ds(h * HEAD_DIM, HEAD_DIM)], kv.at[h, 0, core, part])
    load(vq, q.at[pl.ds(GROUP[0], ROWS)])
    load(tq.at[pl.ds(row_id * TXT_ROWS, TXT_ROWS)], q.at[pl.ds(TEXT, TXT_ROWS)])
    load(tk.at[pl.ds(x * TXT_KEYS, TXT_KEYS)], tkv.at[0, pl.ds(0, TXT_KEYS)])
    load(tv.at[pl.ds(x * TXT_KEYS, TXT_KEYS)], tkv.at[1, pl.ds(0, TXT_KEYS)])

    sent = []

    def remote(src, dst, send, recv, to):
        return pltpu.make_async_remote_copy(
            src_ref=src, dst_ref=dst, send_sem=send, recv_sem=recv,
            device_id=to, device_id_type=MESH)

    def start(copy):
        copy.start()
        sent.append(copy)

    def z_copy(h, part, direction, d):
        here = d - 1 if direction == 0 else (NZ - d + 1) % NZ
        there = d if direction == 0 else NZ - d
        src = kv.at[h, here, core, part]
        if d == 1:
            src = (vk, vv)[part].at[:, pl.ds(h * HEAD_DIM, HEAD_DIM)]
        sems = (h, part, direction, d - 1)
        return remote(src, kv.at[h, there, core, part], z_send.at[sems], z_recv.at[sems],
                      up if direction == 0 else down)

    def s_copy(h, slot, cc):
        ref = kv.at[h, slot, cc]
        return remote(ref, ref, s_send.at[h, slot], s_recv.at[h, slot], sibling)

    def s_own(h, part, cc):
        index = 0 if part == 0 else NZ
        return remote((vk, vv)[part].at[:, pl.ds(h * HEAD_DIM, HEAD_DIM)], kv.at[h, 0, cc, part],
                      s_send.at[h, index], s_recv.at[h, index], sibling)

    def q_copy(k):
        return remote(vq, q.at[pl.ds(GROUP[NX - k], ROWS)], q_send.at[k], q_recv.at[k], x_device(k))

    pl.semaphore_wait(barrier, len(peers))
    for h in range(HEADS):
        for part in range(2):
            for direction in range(2):
                start(z_copy(h, part, direction, 1))
    for k in (2, 1, 3):
        start(q_copy(k))
    for h in range(HEADS):
        for part in range(2):
            start(s_own(h, part, core))
    signal(up_sem.at[0], y_device(1))
    signal(down_sem.at[0], y_device(NY - 1))
    w_loads = []
    for k in range(NY):
        copy = pltpu.make_async_copy(
            w.at[:, pl.ds(((y + k) % NY) * FEATURES, FEATURES)], wbuf.at[k], w_sem.at[k])
        copy.start()
        w_loads.append(copy)

    for s in range(5):
        for half in range(2):
            cols = slice(half * HEAD_DIM, (half + 1) * HEAD_DIM)
            if half == 1 and s == 4:
                continue
            if half == 1 and s == 0:
                lane = lax.broadcasted_iota(jnp.int32, (QUERIES, HEAD_DIM), 1)
                bias[0, :, cols] = jnp.where(lane < TXT_KEYS, 0.0, NEG).astype(F32)
                continue
            tile_z = (z + NZ - s) % NZ if half == 0 else (z + s) % NZ
            for k in range(NX):
                if GROUP[k] >= USED[s]:
                    continue
                reach = mask[z * NX + (x + k) % NX, tile_z * NX + x].astype(F32)
                bias[s, GROUP[k]:GROUP[k] + ROWS, cols] = jnp.full(
                    (ROWS, HEAD_DIM), (1.0 - reach) * NEG, F32)
            bias[s, TEXT:TEXT + TXT_ROWS, cols] = jnp.zeros((TXT_ROWS, HEAD_DIM), F32)
    for part in range(2):
        tkv[part, TXT_KEYS:] = jnp.zeros((HEAD_DIM - TXT_KEYS, FEATURES), BF16)

    ones = jnp.ones((STEP_KEYS, HEAD_DIM), BF16)

    def absorb(h, s):
        cols = slice(h * HEAD_DIM, (h + 1) * HEAD_DIM)
        slots = {0: (0,), 4: (4,)}.get(s, (s, NZ - s))
        used = USED[s]
        keys = [kv[h, slot, cc, 0] for slot in slots for cc in range(2)]
        values = [kv[h, slot, cc, 1] for slot in slots for cc in range(2)]
        if s == 0:
            keys.append(tkv[0, :, cols])
            values.append(tkv[1, :, cols])
        keys, values = jnp.concatenate(keys, 0), jnp.concatenate(values, 0)
        count = keys.shape[0]
        scores = lax.dot_general(q[:used, cols], keys, (((1,), (1,)), ((), ())),
                                 preferred_element_type=F32)
        scores = scores * SCALE + bias[s, :used, :count]
        high = jnp.max(scores, axis=1, keepdims=True)
        if s:
            before = top[h, :used][:, :1]
            high = jnp.maximum(high, before)
        weights = jnp.exp2(scores - high).astype(BF16)
        values = jnp.concatenate([values, ones[:count]], 1)
        summed = jnp.dot(weights, values, preferred_element_type=F32)
        if s:
            summed = summed + acc[h, :used] * jnp.exp2(before - high)
        acc[h, :used] = summed
        top[h, :used] = jnp.broadcast_to(high, (used, HEAD_DIM))

    def forward(h, d):
        if d < 4:
            for part in range(2):
                for direction in range(2):
                    z_copy(h, part, direction, d).wait_recv()
                    if d < 3 or part == direction:
                        start(z_copy(h, part, direction, d + 1))
            for direction in range(2):
                start(s_copy(h, d if direction == 0 else NZ - d, core))
        else:
            for part in range(2):
                z_copy(h, part, part, 4).wait_recv()
            start(s_copy(h, 4, core))

    def from_sibling(h, s):
        if s == 0:
            for part in range(2):
                s_own(h, part, 1 - core).wait_recv()
        else:
            for slot in (s, NZ - s) if s < 4 else (4,):
                s_copy(h, slot, 1 - core).wait_recv()

    def eye(rows):
        return (lax.broadcasted_iota(jnp.int32, (rows, HEAD_DIM), 0)
                == lax.broadcasted_iota(jnp.int32, (rows, HEAD_DIM), 1))

    def finish(h, first, rows):
        block = slice(first, first + rows)
        total = acc[h, block, HEAD_DIM:]
        return acc[h, block, :HEAD_DIM] / total, top[h, block] + jnp.log2(total)

    def to_rows(level):
        row = jnp.sum(jnp.where(eye(level.shape[0]), level, 0.0), axis=0, keepdims=True)
        first = row.astype(BF16).astype(F32)
        second = (row - first).astype(BF16).astype(F32)
        index = lax.broadcasted_iota(jnp.int32, (16, HEAD_DIM), 0)
        rest = jnp.where(index == 1, second, jnp.where(index == 2, row - first - second, 0.0))
        return jnp.where(index == 0, first, rest).astype(BF16)

    def to_column(rows, count):
        row = rows[0:1] + rows[1:2] + rows[2:3]
        return jnp.sum(jnp.where(eye(count), jnp.broadcast_to(row, (count, HEAD_DIM)), 0.0),
                       axis=1, keepdims=True)

    def o_copy(h, k):
        return remote(osend.at[h, k], orecv.at[h, k], o_send.at[h, k], o_recv.at[h, k], x_device(k))

    def give(h, k):
        block, level = finish(h, GROUP[k], ROWS)
        osend[h, k, :ROWS] = block.astype(BF16)
        osend[h, k, ROWS:] = to_rows(level)
        start(o_copy(h, k))

    def merge(parts, levels):
        high = functools.reduce(jnp.maximum, levels)
        shares = [jnp.exp2(level - high) for level in levels]
        total = functools.reduce(jnp.add, shares)
        return functools.reduce(
            jnp.add, [part * (share / total) for part, share in zip(parts, shares)]).astype(BF16)

    for copy in loads:
        copy.wait()
    for k in (1, 3, 2):
        q_copy(k).wait_recv()
    for h in range(HEADS):
        forward(h, 1)
        from_sibling(h, 0)
        absorb(h, 0)
    for step in range(1, 3):
        pl.semaphore_wait(up_sem.at[step - 1], 1)
        pl.semaphore_wait(down_sem.at[step - 1], 1)
        signal(up_sem.at[step], y_device(1))
        signal(down_sem.at[step], y_device(NY - 1))
    for h in range(HEADS):
        forward(h, 2)
        from_sibling(h, 1)
        absorb(h, 1)
        give(h, 2)
    for h in range(HEADS):
        forward(h, 3)
        from_sibling(h, 2)
        absorb(h, 2)
    for h in range(HEADS):
        from_sibling(h, 3)
        absorb(h, 3)
        give(h, 1)
        give(h, 3)
    for h in range(HEADS):
        forward(h, 4)
    pl.semaphore_wait(up_sem.at[2], 1)
    pl.semaphore_wait(down_sem.at[2], 1)
    for copy in w_loads:
        copy.wait()

    for h in range(HEADS):
        from_sibling(h, 4)
        absorb(h, 4)
        part, level = finish(h, TEXT, TXT_ROWS)
        tsend[h, :TXT_ROWS] = part.astype(BF16)
        tsend[h, TXT_ROWS:] = to_rows(level)

    def x_copy(k):
        return remote(tsend, trecv.at[k], x_send.at[k], x_recv.at[k], x_device(k))

    for k in (2, 1, 3):
        start(x_copy(k))

    for h in range(HEADS):
        part, level = finish(h, GROUP[0], ROWS)
        parts, levels = [part], [level[:, :1]]
        for k in (2, 1, 3):
            o_copy(h, k).wait_recv()
            parts.append(orecv[h, k, :ROWS].astype(F32))
            levels.append(to_column(orecv[h, k, ROWS:].astype(F32), ROWS))
        attn[:, h * HEAD_DIM:(h + 1) * HEAD_DIM] = merge(parts, levels)

    def product(k):
        return jnp.dot(attn[...], wbuf[k], preferred_element_type=F32)

    def y_copy(k):
        to = {3: 1, 5: NY - 1}.get(k, k)
        return remote(ysend.at[k], yrecv.at[k], y_send.at[k], y_recv.at[k], y_device(to))

    for k in (3, 5, 4):
        ysend[k] = product(k).astype(BF16)
        start(y_copy(k))
    for k in (1, 7):
        ysend[k] = product(k).astype(BF16)
    for k, relay in ((2, 3), (6, 5)):
        yterm[...] = product(k)
        y_copy(relay).wait_recv()
        yterm[...] += yrecv[relay].astype(F32)
        ysend[k] = yterm[...].astype(BF16)
        start(y_copy(k))
    for k in (1, 7):
        start(y_copy(k))
    total = product(0)

    mine = pl.ds(pl.multiple_of(row_id * TXT_ROWS, TXT_ROWS), TXT_ROWS)
    for k in (1, 2, 3):
        x_copy(k).wait_recv()
    trecv[0] = tsend[...]
    for h in range(HEADS):
        parts = [trecv[k, h, :TXT_ROWS].astype(F32) for k in range(NX)]
        levels = [to_column(trecv[k, h, TXT_ROWS:].astype(F32), TXT_ROWS) for k in range(NX)]
        tout[mine, h * HEAD_DIM:(h + 1) * HEAD_DIM] = merge(parts, levels)
    for k in range(1, 2 * NZ):
        start(remote(tout.at[mine], tout.at[mine], t_send.at[k], t_recv.at[k], text_device(k)))

    for k in (4, 1, 7, 2, 6):
        y_copy(k).wait_recv()
        total = total + yrecv[k].astype(F32)
    out[...] = total.astype(BF16)

    for k in range(1, 2 * NZ):
        other = (row_id + 2 * NZ - k) % (2 * NZ)
        ref = tout.at[pl.ds(pl.multiple_of(other * TXT_ROWS, TXT_ROWS), TXT_ROWS)]
        remote(ref, ref, t_send.at[k], t_recv.at[k], text_device(k)).wait_recv()
    for copy in sent:
        copy.wait_send()


def local(video_q, video_k, video_v, text_q, text_k, text_v, tile_mask, out_weight):
    hbm = pl.BlockSpec(memory_space=pltpu.HBM)
    vmem = pl.BlockSpec(memory_space=pltpu.VMEM)
    dma = pltpu.SemaphoreType.DMA
    regular = pltpu.SemaphoreType.REGULAR
    return pl.pallas_call(
        body,
        out_shape=(
            jax.ShapeDtypeStruct((ROWS, FEATURES), BF16),
            jax.ShapeDtypeStruct((2 * NZ * TXT_ROWS, FEATURES), BF16),
        ),
        in_specs=[hbm] * 6 + [pl.BlockSpec(memory_space=pltpu.SMEM), hbm],
        out_specs=(vmem, vmem),
        scratch_shapes=[
            pltpu.VMEM((QUERIES, FEATURES), BF16),
            pltpu.VMEM((HEADS, NZ, 2, 2, ROWS, HEAD_DIM), BF16),
            pltpu.VMEM((2, HEAD_DIM, FEATURES), BF16),
            pltpu.VMEM((5, QUERIES, STEP_KEYS), F32),
            pltpu.VMEM((HEADS, QUERIES, 2 * HEAD_DIM), F32),
            pltpu.VMEM((HEADS, QUERIES, HEAD_DIM), F32),
            pltpu.VMEM((HEADS, NX, ROWS + 16, HEAD_DIM), BF16),
            pltpu.VMEM((HEADS, NX, ROWS + 16, HEAD_DIM), BF16),
            pltpu.VMEM((HEADS, TXT_ROWS + 16, HEAD_DIM), BF16),
            pltpu.VMEM((NX, HEADS, TXT_ROWS + 16, HEAD_DIM), BF16),
            pltpu.VMEM((ROWS, FEATURES), BF16),
            pltpu.VMEM((NY, FEATURES, FEATURES), BF16),
            pltpu.VMEM((NY, ROWS, FEATURES), BF16),
            pltpu.VMEM((NY, ROWS, FEATURES), BF16),
            pltpu.VMEM((ROWS, FEATURES), F32),
            dma((10,)),
            dma((NY,)),
            dma((NX,)), dma((NX,)),
            dma((HEADS, 2, 2, 4)), dma((HEADS, 2, 2, 4)),
            dma((HEADS, NZ + 1)), dma((HEADS, NZ + 1)),
            dma((HEADS, NX)), dma((HEADS, NX)),
            dma((NX,)), dma((NX,)),
            dma((NY,)), dma((NY,)),
            dma((2 * NZ,)), dma((2 * NZ,)),
            regular((3,)), regular((3,)),
        ],
        compiler_params=pltpu.CompilerParams(
            collective_id=0, has_side_effects=True, vmem_limit_bytes=60 * 2**20),
    )(video_q, video_k, video_v, text_q, text_k, text_v, tile_mask, out_weight)


def solution(mesh):
    placed = (
        P("ctx", "head"),
        P("ctx", "head"),
        P("ctx", "head"),
        P(None, "head"),
        P(None, "head"),
        P(None, "head"),
        P(),
        P("head", None),
    )
    return jax.shard_map(
        local,
        mesh=mesh,
        in_specs=placed,
        out_specs=(P("ctx", "head"), P(None, "head")),
        check_vma=False,
    )
```

```python
import functools
import math

import jax
import jax.numpy as jnp
from jax import lax
from jax.experimental import pallas as pl
from jax.experimental.pallas import tpu as pltpu
from jax.sharding import PartitionSpec as P

HEAD_DIM = 128
ROWS = 64
HEADS = 3
NZ, NX, NY = 8, 4, 8
FEATURES = HEADS * HEAD_DIM
TXT_ROWS = 16
TXT_KEYS = 64
TEXT = 64
GROUP = {0: 0, 1: 80, 3: 144, 2: 208}
QUERIES = 272
USED = (272, 272, 208, 208, 80)
STEP_KEYS = 256
TILES = NZ * NX
PLACE = {3: 0, 5: 1, 1: 2, 2: 3, 4: 4, 6: 5, 7: 6}
NEG = -1e30
SCALE = math.log2(math.e) / math.sqrt(HEAD_DIM)
MESH = pl.DeviceIdType.MESH
BF16, F32 = jnp.bfloat16, jnp.float32


def body(vq, vk, vv, tq, tk, tv, mask, w, out, tout,
         q, kv, tkv, bias, acc, top, osend, orecv, tsend, trecv, attn, wbuf, ysend, yrecv, yterm,
         reach, load_sem, send_sem, z_recv, s_recv, o_recv, once_recv, up_sem, down_sem):
    ctx, y = lax.axis_index("ctx"), lax.axis_index("head")
    core, x, z = ctx % 2, (ctx // 2) % NX, ctx // (2 * NX)
    row_id = 2 * z + core

    def device(zz, xx, cc, yy):
        return ((zz * NX + xx) * 2 + cc, yy)

    def text_device(k):
        other = (row_id + k) % (2 * NZ)
        return device(other // 2, x, other % 2, y)

    up = device((z + 1) % NZ, x, core, y)
    down = device((z + NZ - 1) % NZ, x, core, y)
    sibling = device(z, x, 1 - core, y)

    def x_device(k):
        return device(z, (x + k) % NX, core, y)

    def y_device(k):
        return (ctx, (y + k) % NY)

    def signal(sem, to):
        pl.semaphore_signal(sem, inc=1, device_id=to, device_id_type=MESH)

    barrier = pltpu.get_barrier_semaphore()
    peers = [up, down, sibling] + [x_device(k) for k in range(1, NX)]
    peers += [y_device(1), y_device(NY - 1)]
    for peer in peers:
        signal(barrier, peer)

    def load(src, dst, sem):
        pltpu.make_async_copy(src, dst, load_sem.at[sem]).start()

    def take(ref, sem):
        pltpu.make_async_copy(ref, ref, sem).wait()

    def remote(src, dst, send, recv, to):
        return pltpu.make_async_remote_copy(
            src_ref=src, dst_ref=dst, send_sem=send, recv_sem=recv,
            device_id=to, device_id_type=MESH)

    def slot(direction, d):
        return {0: 0, 4: 1}.get(d, 2 * d + direction)

    def z_copy(h, part, direction, d):
        src = kv.at[h, slot(direction, d - 1), core]
        dst = kv.at[h, slot(direction, d), core]
        if part is not None:
            src, dst = src.at[part], dst.at[part]
        if d == 1:
            src = (vk, vv)[part].at[:, pl.ds(h * HEAD_DIM, HEAD_DIM)]
        return remote(src, dst, send_sem.at[0], z_recv.at[h, direction, d - 1],
                      up if direction == 0 else down)

    def s_copy(h, place, step):
        ref = kv.at[h, place, core]
        return remote(ref, ref, send_sem.at[1], s_recv.at[h, step], sibling)

    def s_own(h, part):
        return remote((vk, vv)[part].at[:, pl.ds(h * HEAD_DIM, HEAD_DIM)], kv.at[h, 0, core, part],
                      send_sem.at[1], s_recv.at[h, 0], sibling)

    def q_copy(k):
        return remote(vq, q.at[pl.ds(GROUP[NX - k], ROWS)], send_sem.at[2], once_recv.at[0],
                      x_device(k))

    pl.semaphore_wait(barrier, len(peers))
    for h in range(HEADS):
        for direction in range(2):
            z_copy(h, 0, direction, 1).start()
            z_copy(h, 1, direction, 1).start()
    for k in (2, 1, 3):
        q_copy(k).start()
    for h in range(HEADS):
        for part in range(2):
            s_own(h, part).start()
    load(mask, reach, 0)
    for h in range(HEADS):
        for part, ref in enumerate((vk, vv)):
            load(ref.at[:, pl.ds(h * HEAD_DIM, HEAD_DIM)], kv.at[h, 0, core, part], 1)
    load(vq, q.at[pl.ds(GROUP[0], ROWS)], 2)
    load(tq.at[pl.ds(row_id * TXT_ROWS, TXT_ROWS)], q.at[pl.ds(TEXT, TXT_ROWS)], 3)
    for part, ref in enumerate((tk, tv)):
        load(ref.at[pl.ds(x * TXT_KEYS, TXT_KEYS)], tkv.at[part, pl.ds(0, TXT_KEYS)], 4)
    signal(up_sem.at[0], y_device(1))
    signal(down_sem.at[0], y_device(NY - 1))
    for k in range(NY):
        load(w.at[:, pl.ds(((y + k) % NY) * FEATURES, FEATURES)], wbuf.at[k], 5)
    take(reach, load_sem.at[0])

    for s in range(5):
        for half in range(2):
            cols = slice(half * HEAD_DIM, (half + 1) * HEAD_DIM)
            if half == 1 and s == 4:
                continue
            if half == 1 and s == 0:
                lane = lax.broadcasted_iota(jnp.int32, (QUERIES, HEAD_DIM), 1)
                bias[0, :, cols] = jnp.where(lane < TXT_KEYS, 0.0, NEG).astype(F32)
                continue
            tile_z = (z + NZ - s) % NZ if half == 0 else (z + s) % NZ
            for k in range(NX):
                if GROUP[k] >= USED[s]:
                    continue
                allowed = reach[z * NX + (x + k) % NX, tile_z * NX + x].astype(F32)
                bias[s, GROUP[k]:GROUP[k] + ROWS, cols] = jnp.full(
                    (ROWS, HEAD_DIM), (1.0 - allowed) * NEG, F32)
            bias[s, TEXT:TEXT + TXT_ROWS, cols] = jnp.zeros((TXT_ROWS, HEAD_DIM), F32)
    for part in range(2):
        tkv[part, TXT_KEYS:] = jnp.zeros((HEAD_DIM - TXT_KEYS, FEATURES), BF16)

    ones = jnp.ones((STEP_KEYS, HEAD_DIM), BF16)

    def absorb(h, s):
        cols = slice(h * HEAD_DIM, (h + 1) * HEAD_DIM)
        slots = {0: (0,), 4: (1,)}.get(s, (2 * s, 2 * s + 1))
        used = USED[s]
        keys = [kv[h, slot, cc, 0] for slot in slots for cc in range(2)]
        values = [kv[h, slot, cc, 1] for slot in slots for cc in range(2)]
        if s == 0:
            keys.append(tkv[0, :, cols])
            values.append(tkv[1, :, cols])
        keys, values = jnp.concatenate(keys, 0), jnp.concatenate(values, 0)
        count = keys.shape[0]
        scores = lax.dot_general(q[:used, cols], keys, (((1,), (1,)), ((), ())),
                                 preferred_element_type=F32)
        scores = scores * SCALE + bias[s, :used, :count]
        high = jnp.max(scores, axis=1, keepdims=True)
        if s:
            before = top[h, :used][:, :1]
            high = jnp.maximum(high, before)
        weights = jnp.exp2(scores - high).astype(BF16)
        values = jnp.concatenate([values, ones[:count]], 1)
        summed = jnp.dot(weights, values, preferred_element_type=F32)
        if s:
            summed = summed + acc[h, :used] * jnp.exp2(before - high)
        acc[h, :used] = summed
        top[h, :used] = jnp.broadcast_to(high, (used, HEAD_DIM))

    def forward(h, d):
        for direction in range(2):
            if d < 4:
                ref = kv.at[h, slot(direction, d), core]
            else:
                ref = kv.at[h, 1, core, direction]
            take(ref, z_recv.at[h, direction, d - 1])
            if d < 4:
                z_copy(h, direction if d == 3 else None, direction, d + 1).start()
        for place in (slot(0, d), slot(1, d)) if d < 4 else (1,):
            s_copy(h, place, d).start()

    def from_sibling(h, s):
        places = {0: 0, 4: 1}.get(s, pl.ds(2 * s, 2))
        take(kv.at[h, places, 1 - core], s_recv.at[h, s])

    def eye(rows):
        return (lax.broadcasted_iota(jnp.int32, (rows, HEAD_DIM), 0)
                == lax.broadcasted_iota(jnp.int32, (rows, HEAD_DIM), 1))

    def finish(h, first, rows):
        block = slice(first, first + rows)
        total = acc[h, block, HEAD_DIM:]
        return acc[h, block, :HEAD_DIM] / total, top[h, block] + jnp.log2(total)

    def to_rows(level):
        row = jnp.sum(jnp.where(eye(level.shape[0]), level, 0.0), axis=0, keepdims=True)
        first = row.astype(BF16).astype(F32)
        second = (row - first).astype(BF16).astype(F32)
        index = lax.broadcasted_iota(jnp.int32, (16, HEAD_DIM), 0)
        rest = jnp.where(index == 1, second, jnp.where(index == 2, row - first - second, 0.0))
        return jnp.where(index == 0, first, rest).astype(BF16)

    def to_column(rows, count):
        row = rows[0:1] + rows[1:2] + rows[2:3]
        return jnp.sum(jnp.where(eye(count), jnp.broadcast_to(row, (count, HEAD_DIM)), 0.0),
                       axis=1, keepdims=True)

    def o_copy(h, k):
        return remote(osend.at[h, k - 1], orecv.at[h, k - 1], send_sem.at[3], o_recv.at[h, k - 1],
                      x_device(k))

    def give(h, k):
        block, level = finish(h, GROUP[k], ROWS)
        osend[h, k - 1, :ROWS] = block.astype(BF16)
        osend[h, k - 1, ROWS:] = to_rows(level)
        o_copy(h, k).start()

    def merge(parts, levels):
        high = functools.reduce(jnp.maximum, levels)
        shares = [jnp.exp2(level - high) for level in levels]
        total = functools.reduce(jnp.add, shares)
        return functools.reduce(
            jnp.add, [part * (share / total) for part, share in zip(parts, shares)]).astype(BF16)

    take(kv.at[:, 0, core], load_sem.at[1])
    take(q.at[pl.ds(GROUP[0], ROWS)], load_sem.at[2])
    take(q.at[pl.ds(TEXT, TXT_ROWS)], load_sem.at[3])
    take(tkv.at[:, pl.ds(0, TXT_KEYS)], load_sem.at[4])
    take(q.at[pl.ds(GROUP[1], 3 * ROWS)], once_recv.at[0])
    for h in range(HEADS):
        forward(h, 1)
        from_sibling(h, 0)
        absorb(h, 0)
    for step in range(1, 3):
        pl.semaphore_wait(up_sem.at[step - 1], 1)
        pl.semaphore_wait(down_sem.at[step - 1], 1)
        signal(up_sem.at[step], y_device(1))
        signal(down_sem.at[step], y_device(NY - 1))
    for h in range(HEADS):
        forward(h, 2)
        from_sibling(h, 1)
        absorb(h, 1)
        give(h, 2)
    for h in range(HEADS):
        forward(h, 3)
        from_sibling(h, 2)
        absorb(h, 2)
    for h in range(HEADS):
        from_sibling(h, 3)
        absorb(h, 3)
        give(h, 1)
        give(h, 3)
    for h in range(HEADS):
        forward(h, 4)
    pl.semaphore_wait(up_sem.at[2], 1)
    pl.semaphore_wait(down_sem.at[2], 1)
    take(wbuf, load_sem.at[5])

    for h in range(HEADS):
        from_sibling(h, 4)
    for h in range(HEADS):
        absorb(h, 4)
    for h in range(HEADS):
        for k in range(1, NX):
            o_copy(h, k).wait_recv()

    for h in range(HEADS):
        part, level = finish(h, GROUP[0], ROWS)
        parts, levels = [part], [level[:, :1]]
        for k in range(1, NX):
            parts.append(orecv[h, k - 1, :ROWS].astype(F32))
            levels.append(to_column(orecv[h, k - 1, ROWS:].astype(F32), ROWS))
        attn[:, h * HEAD_DIM:(h + 1) * HEAD_DIM] = merge(parts, levels)

    def product(k):
        return jnp.dot(attn[...], wbuf[k], preferred_element_type=F32)

    def y_copy(k):
        to = {3: 1, 5: NY - 1}.get(k, k)
        return remote(ysend.at[PLACE[k]], yrecv.at[PLACE[k]], send_sem.at[5],
                      once_recv.at[{3: 2, 5: 3}.get(k, 4)], y_device(to))

    for k in (3, 5, 4, 1, 7):
        ysend[PLACE[k]] = product(k).astype(BF16)
        y_copy(k).start()

    def x_copy(k):
        return remote(tsend, trecv.at[k], send_sem.at[4], once_recv.at[1], x_device(k))

    for h in range(HEADS):
        part, level = finish(h, TEXT, TXT_ROWS)
        tsend[h, :TXT_ROWS] = part.astype(BF16)
        tsend[h, TXT_ROWS:] = to_rows(level)
    for k in (2, 1, 3):
        x_copy(k).start()
    for k, relay in ((2, 3), (6, 5)):
        yterm[...] = product(k)
        y_copy(relay).wait_recv()
        yterm[...] += yrecv[PLACE[relay]].astype(F32)
        ysend[PLACE[k]] = yterm[...].astype(BF16)
        y_copy(k).start()
    total = product(0)

    mine = pl.ds(pl.multiple_of(row_id * TXT_ROWS, TXT_ROWS), TXT_ROWS)
    take(trecv.at[pl.ds(1, NX - 1)], once_recv.at[1])
    trecv[0] = tsend[...]
    for h in range(HEADS):
        parts = [trecv[k, h, :TXT_ROWS].astype(F32) for k in range(NX)]
        levels = [to_column(trecv[k, h, TXT_ROWS:].astype(F32), TXT_ROWS) for k in range(NX)]
        tout[mine, h * HEAD_DIM:(h + 1) * HEAD_DIM] = merge(parts, levels)
    for k in range(1, 2 * NZ):
        remote(tout.at[mine], tout.at[mine], send_sem.at[6], once_recv.at[5], text_device(k)).start()

    take(yrecv.at[pl.ds(2, 5)], once_recv.at[4])
    for k in (1, 2, 4, 6, 7):
        total = total + yrecv[PLACE[k]].astype(F32)
    out[...] = total.astype(BF16)

    rest = tout.at[pl.ds(0, (2 * NZ - 1) * TXT_ROWS)]
    take(rest, once_recv.at[5])
    for index, ref in enumerate((kv.at[:, pl.ds(0, 7), 0], kv.at[:, :, 0],
                                 q.at[pl.ds(GROUP[1], 3 * ROWS)], osend,
                                 trecv.at[pl.ds(1, NX - 1)], ysend, rest)):
        take(ref, send_sem.at[index])


def local(video_q, video_k, video_v, text_q, text_k, text_v, tile_mask, out_weight):
    hbm = pl.BlockSpec(memory_space=pltpu.HBM)
    vmem = pl.BlockSpec(memory_space=pltpu.VMEM)
    dma = pltpu.SemaphoreType.DMA
    in_hbm = functools.partial(pltpu.with_memory_space_constraint, memory_space=pltpu.HBM)
    regular = pltpu.SemaphoreType.REGULAR
    return pl.pallas_call(
        body,
        out_shape=(
            jax.ShapeDtypeStruct((ROWS, FEATURES), BF16),
            jax.ShapeDtypeStruct((2 * NZ * TXT_ROWS, FEATURES), BF16),
        ),
        in_specs=[hbm] * 6 + [hbm, hbm],
        out_specs=(vmem, vmem),
        scratch_shapes=[
            pltpu.VMEM((QUERIES, FEATURES), BF16),
            pltpu.VMEM((HEADS, NZ, 2, 2, ROWS, HEAD_DIM), BF16),
            pltpu.VMEM((2, HEAD_DIM, FEATURES), BF16),
            pltpu.VMEM((5, QUERIES, STEP_KEYS), F32),
            pltpu.VMEM((HEADS, QUERIES, 2 * HEAD_DIM), F32),
            pltpu.VMEM((HEADS, QUERIES, HEAD_DIM), F32),
            pltpu.VMEM((HEADS, NX - 1, ROWS + 16, HEAD_DIM), BF16),
            pltpu.VMEM((HEADS, NX - 1, ROWS + 16, HEAD_DIM), BF16),
            pltpu.VMEM((HEADS, TXT_ROWS + 16, HEAD_DIM), BF16),
            pltpu.VMEM((NX, HEADS, TXT_ROWS + 16, HEAD_DIM), BF16),
            pltpu.VMEM((ROWS, FEATURES), BF16),
            pltpu.VMEM((NY, FEATURES, FEATURES), BF16),
            pltpu.VMEM((NY - 1, ROWS, FEATURES), BF16),
            pltpu.VMEM((NY - 1, ROWS, FEATURES), BF16),
            pltpu.VMEM((ROWS, FEATURES), F32),
            pltpu.SMEM((TILES, TILES), jnp.int32),
            dma((6,)),
            dma((7,)),
            dma((HEADS, 2, 4)),
            dma((HEADS, 5)),
            dma((HEADS, NX - 1)),
            dma((6,)),
            regular((3,)), regular((3,)),
        ],
        compiler_params=pltpu.CompilerParams(
            collective_id=0, has_side_effects=True, vmem_limit_bytes=40 * 2**20),
    )(*map(in_hbm, (video_q, video_k, video_v, text_q, text_k, text_v, tile_mask, out_weight)))


def solution(mesh):
    placed = (
        P("ctx", "head"),
        P("ctx", "head"),
        P("ctx", "head"),
        P(None, "head"),
        P(None, "head"),
        P(None, "head"),
        P(),
        P("head", None),
    )
    return jax.shard_map(
        local,
        mesh=mesh,
        in_specs=placed,
        out_specs=(P("ctx", "head"), P(None, "head")),
        check_vma=False,
    )
```

```python
import functools
import math

import jax
import jax.numpy as jnp
from jax import lax
from jax.experimental import pallas as pl
from jax.experimental.pallas import tpu as pltpu
from jax.sharding import PartitionSpec as P

HEAD_DIM = 128
ROWS = 64
HEADS = 3
NZ, NX, NY = 8, 4, 8
FEATURES = HEADS * HEAD_DIM
TXT_ROWS = 16
TXT_KEYS = 64
TEXT = 64
GROUP = {0: 0, 1: 80, 3: 144, 2: 208}
QUERIES = 272
USED = (272, 272, 208, 208, 80)
STEP_KEYS = 256
TILES = NZ * NX
PLACE = {3: 0, 5: 1, 1: 2, 2: 3, 4: 4, 6: 5, 7: 6}
NEG = -1e30
SCALE = math.log2(math.e) / math.sqrt(HEAD_DIM)
MESH = pl.DeviceIdType.MESH
BF16, F32 = jnp.bfloat16, jnp.float32


def body(vq, vk, vv, tq, tk, tv, mask, w, out, tout,
         q, kv, tkv, bias, acc, top, osend, orecv, tsend, trecv, attn, wbuf, ysend, yrecv, yterm,
         reach, load_sem, send_sem, z_recv, s_recv, o_recv, once_recv, up_sem, down_sem):
    ctx, y = lax.axis_index("ctx"), lax.axis_index("head")
    core, x, z = ctx % 2, (ctx // 2) % NX, ctx // (2 * NX)
    row_id = 2 * z + core

    def device(zz, xx, cc, yy):
        return ((zz * NX + xx) * 2 + cc, yy)

    def text_device(k):
        other = (row_id + k) % (2 * NZ)
        return device(other // 2, x, other % 2, y)

    up = device((z + 1) % NZ, x, core, y)
    down = device((z + NZ - 1) % NZ, x, core, y)
    sibling = device(z, x, 1 - core, y)

    def x_device(k):
        return device(z, (x + k) % NX, core, y)

    def y_device(k):
        return (ctx, (y + k) % NY)

    def signal(sem, to):
        pl.semaphore_signal(sem, inc=1, device_id=to, device_id_type=MESH)

    barrier = pltpu.get_barrier_semaphore()
    peers = [up, down, sibling] + [x_device(k) for k in range(1, NX)]
    peers += [y_device(1), y_device(NY - 1)]
    for peer in peers:
        signal(barrier, peer)

    def load(src, dst, sem):
        pltpu.make_async_copy(src, dst, load_sem.at[sem]).start()

    def take(ref, sem):
        pltpu.make_async_copy(ref, ref, sem).wait()

    def remote(src, dst, send, recv, to):
        return pltpu.make_async_remote_copy(
            src_ref=src, dst_ref=dst, send_sem=send, recv_sem=recv,
            device_id=to, device_id_type=MESH)

    def slot(direction, d):
        return {0: 0, 4: 1}.get(d, 2 * d + direction)

    def z_copy(h, part, direction, d):
        src = kv.at[h, slot(direction, d - 1), core]
        dst = kv.at[h, slot(direction, d), core]
        if part is not None:
            src, dst = src.at[part], dst.at[part]
        if d == 1:
            src = (vk, vv)[part].at[:, pl.ds(h * HEAD_DIM, HEAD_DIM)]
        return remote(src, dst, send_sem.at[0], z_recv.at[h, direction, d - 1],
                      up if direction == 0 else down)

    def s_copy(h, place, step):
        ref = kv.at[h, place, core]
        return remote(ref, ref, send_sem.at[1], s_recv.at[h, step], sibling)

    def s_own(h, part):
        return remote((vk, vv)[part].at[:, pl.ds(h * HEAD_DIM, HEAD_DIM)], kv.at[h, 0, core, part],
                      send_sem.at[1], s_recv.at[h, 0], sibling)

    def q_copy(k):
        return remote(vq, q.at[pl.ds(GROUP[NX - k], ROWS)], send_sem.at[2], once_recv.at[0],
                      x_device(k))

    pl.semaphore_wait(barrier, len(peers))
    for h in range(HEADS):
        for direction in range(2):
            z_copy(h, 0, direction, 1).start()
            z_copy(h, 1, direction, 1).start()
    for k in (2, 1, 3):
        q_copy(k).start()
    for h in range(HEADS):
        for part in range(2):
            s_own(h, part).start()
    load(mask, reach, 0)
    for h in range(HEADS):
        for part, ref in enumerate((vk, vv)):
            load(ref.at[:, pl.ds(h * HEAD_DIM, HEAD_DIM)], kv.at[h, 0, core, part], 1)
    load(vq, q.at[pl.ds(GROUP[0], ROWS)], 2)
    load(tq.at[pl.ds(row_id * TXT_ROWS, TXT_ROWS)], q.at[pl.ds(TEXT, TXT_ROWS)], 3)
    for part, ref in enumerate((tk, tv)):
        load(ref.at[pl.ds(x * TXT_KEYS, TXT_KEYS)], tkv.at[part, pl.ds(0, TXT_KEYS)], 4)
    signal(up_sem.at[0], y_device(1))
    signal(down_sem.at[0], y_device(NY - 1))
    for k in range(NY):
        load(w.at[:, pl.ds(((y + k) % NY) * FEATURES, FEATURES)], wbuf.at[k], 5)
    take(reach, load_sem.at[0])

    for s in range(5):
        for half in range(2):
            cols = slice(half * HEAD_DIM, (half + 1) * HEAD_DIM)
            if half == 1 and s == 4:
                continue
            if half == 1 and s == 0:
                lane = lax.broadcasted_iota(jnp.int32, (QUERIES, HEAD_DIM), 1)
                bias[0, :, cols] = jnp.where(lane < TXT_KEYS, 0.0, NEG).astype(F32)
                continue
            tile_z = (z + NZ - s) % NZ if half == 0 else (z + s) % NZ
            for k in range(NX):
                if GROUP[k] >= USED[s]:
                    continue
                allowed = reach[z * NX + (x + k) % NX, tile_z * NX + x].astype(F32)
                bias[s, GROUP[k]:GROUP[k] + ROWS, cols] = jnp.full(
                    (ROWS, HEAD_DIM), (1.0 - allowed) * NEG, F32)
            bias[s, TEXT:TEXT + TXT_ROWS, cols] = jnp.zeros((TXT_ROWS, HEAD_DIM), F32)
    for part in range(2):
        tkv[part, TXT_KEYS:] = jnp.zeros((HEAD_DIM - TXT_KEYS, FEATURES), BF16)

    ones = jnp.ones((STEP_KEYS, HEAD_DIM), BF16)

    def absorb(h, s):
        cols = slice(h * HEAD_DIM, (h + 1) * HEAD_DIM)
        slots = {0: (0,), 4: (1,)}.get(s, (2 * s, 2 * s + 1))
        used = USED[s]
        keys = [kv[h, slot, cc, 0] for slot in slots for cc in range(2)]
        values = [kv[h, slot, cc, 1] for slot in slots for cc in range(2)]
        if s == 0:
            keys.append(tkv[0, :, cols])
            values.append(tkv[1, :, cols])
        keys, values = jnp.concatenate(keys, 0), jnp.concatenate(values, 0)
        count = keys.shape[0]
        scores = lax.dot_general(q[:used, cols], keys, (((1,), (1,)), ((), ())),
                                 preferred_element_type=F32)
        scores = scores * SCALE + bias[s, :used, :count]
        high = jnp.max(scores, axis=1, keepdims=True)
        if s:
            before = top[h, :used][:, :1]
            high = jnp.maximum(high, before)
        weights = jnp.exp2(scores - high).astype(BF16)
        values = jnp.concatenate([values, ones[:count]], 1)
        summed = jnp.dot(weights, values, preferred_element_type=F32)
        if s:
            summed = summed + acc[h, :used] * jnp.exp2(before - high)
        acc[h, :used] = summed
        top[h, :used] = jnp.broadcast_to(high, (used, HEAD_DIM))

    def forward(h, d):
        for direction in range(2):
            if d < 4:
                ref = kv.at[h, slot(direction, d), core]
            else:
                ref = kv.at[h, 1, core, direction]
            take(ref, z_recv.at[h, direction, d - 1])
            if d < 4:
                z_copy(h, direction if d == 3 else None, direction, d + 1).start()
        for place in (slot(0, d), slot(1, d)) if d < 4 else (1,):
            s_copy(h, place, d).start()

    def from_sibling(h, s):
        places = {0: 0, 4: 1}.get(s, pl.ds(2 * s, 2))
        take(kv.at[h, places, 1 - core], s_recv.at[h, s])

    def eye(rows):
        return (lax.broadcasted_iota(jnp.int32, (rows, HEAD_DIM), 0)
                == lax.broadcasted_iota(jnp.int32, (rows, HEAD_DIM), 1))

    def finish(h, first, rows):
        block = slice(first, first + rows)
        total = acc[h, block, HEAD_DIM:]
        return acc[h, block, :HEAD_DIM] / total, top[h, block] + jnp.log2(total)

    def to_rows(level):
        row = jnp.sum(jnp.where(eye(level.shape[0]), level, 0.0), axis=0, keepdims=True)
        first = row.astype(BF16).astype(F32)
        second = (row - first).astype(BF16).astype(F32)
        index = lax.broadcasted_iota(jnp.int32, (16, HEAD_DIM), 0)
        rest = jnp.where(index == 1, second, jnp.where(index == 2, row - first - second, 0.0))
        return jnp.where(index == 0, first, rest).astype(BF16)

    def to_column(rows, count):
        row = rows[0:1] + rows[1:2] + rows[2:3]
        return jnp.sum(jnp.where(eye(count), jnp.broadcast_to(row, (count, HEAD_DIM)), 0.0),
                       axis=1, keepdims=True)

    def o_copy(h, k):
        return remote(osend.at[h, k - 1], orecv.at[h, k - 1], send_sem.at[3], o_recv.at[h, k - 1],
                      x_device(k))

    def give(h, k):
        block, level = finish(h, GROUP[k], ROWS)
        osend[h, k - 1, :ROWS] = block.astype(BF16)
        osend[h, k - 1, ROWS:] = to_rows(level)
        o_copy(h, k).start()

    def fold(h):
        own = slice(GROUP[0], GROUP[0] + ROWS)
        before = top[h, own][:, :1]
        parts, levels = [acc[h, own]], [before]
        for k in range(1, NX):
            part = orecv[h, k - 1, :ROWS].astype(F32)
            parts.append(jnp.concatenate([part, jnp.ones((ROWS, HEAD_DIM), F32)], 1))
            levels.append(to_column(orecv[h, k - 1, ROWS:].astype(F32), ROWS))
        high = functools.reduce(jnp.maximum, levels)
        acc[h, own] = functools.reduce(
            jnp.add, [part * jnp.exp2(level - high) for part, level in zip(parts, levels)])
        top[h, own] = jnp.broadcast_to(high, (ROWS, HEAD_DIM))

    def merge(parts, levels):
        high = functools.reduce(jnp.maximum, levels)
        shares = [jnp.exp2(level - high) for level in levels]
        total = functools.reduce(jnp.add, shares)
        return functools.reduce(
            jnp.add, [part * (share / total) for part, share in zip(parts, shares)]).astype(BF16)

    for h in range(HEADS):
        forward(h, 1)
    take(kv.at[:, 0, core], load_sem.at[1])
    take(q.at[pl.ds(GROUP[0], ROWS)], load_sem.at[2])
    take(q.at[pl.ds(TEXT, TXT_ROWS)], load_sem.at[3])
    take(tkv.at[:, pl.ds(0, TXT_KEYS)], load_sem.at[4])
    take(q.at[pl.ds(GROUP[1], 3 * ROWS)], once_recv.at[0])
    for h in range(HEADS):
        from_sibling(h, 0)
        absorb(h, 0)
    for h in range(HEADS):
        forward(h, 2)
        from_sibling(h, 1)
        absorb(h, 1)
        give(h, 2)
    pl.semaphore_wait(up_sem.at[0], 1)
    pl.semaphore_wait(down_sem.at[0], 1)
    signal(up_sem.at[1], y_device(1))
    signal(down_sem.at[1], y_device(NY - 1))
    for h in range(HEADS):
        forward(h, 3)
        from_sibling(h, 2)
        absorb(h, 2)
    pl.semaphore_wait(up_sem.at[1], 1)
    pl.semaphore_wait(down_sem.at[1], 1)
    signal(up_sem.at[2], y_device(1))
    signal(down_sem.at[2], y_device(NY - 1))
    for h in range(HEADS):
        from_sibling(h, 3)
        absorb(h, 3)
        give(h, 1)
        give(h, 3)
    for h in range(HEADS):
        forward(h, 4)
    pl.semaphore_wait(up_sem.at[2], 1)
    pl.semaphore_wait(down_sem.at[2], 1)
    take(wbuf, load_sem.at[5])

    for h in range(HEADS):
        for k in range(1, NX):
            o_copy(h, k).wait_recv()
    for h in range(HEADS):
        fold(h)
    for h in range(HEADS):
        from_sibling(h, 4)
    for h in range(HEADS):
        absorb(h, 4)
    own = slice(GROUP[0], GROUP[0] + ROWS)
    for h in range(HEADS):
        attn[:, h * HEAD_DIM:(h + 1) * HEAD_DIM] = (
            acc[h, own, :HEAD_DIM] / acc[h, own, HEAD_DIM:]).astype(BF16)

    def product(k):
        return jnp.dot(attn[...], wbuf[k], preferred_element_type=F32)

    def y_copy(k):
        to = {3: 1, 5: NY - 1}.get(k, k)
        return remote(ysend.at[PLACE[k]], yrecv.at[PLACE[k]], send_sem.at[5],
                      once_recv.at[{3: 2, 5: 3}.get(k, 4)], y_device(to))

    for k in (3, 5, 4, 1, 7):
        ysend[PLACE[k]] = product(k).astype(BF16)
        y_copy(k).start()

    def x_copy(k):
        return remote(tsend, trecv.at[k], send_sem.at[4], once_recv.at[1], x_device(k))

    for h in range(HEADS):
        part, level = finish(h, TEXT, TXT_ROWS)
        tsend[h, :TXT_ROWS] = part.astype(BF16)
        tsend[h, TXT_ROWS:] = to_rows(level)
    for k in (2, 1, 3):
        x_copy(k).start()
    for k, relay in ((2, 3), (6, 5)):
        yterm[...] = product(k)
        y_copy(relay).wait_recv()
        yterm[...] += yrecv[PLACE[relay]].astype(F32)
        ysend[PLACE[k]] = yterm[...].astype(BF16)
        y_copy(k).start()
    total = product(0)

    mine = pl.ds(pl.multiple_of(row_id * TXT_ROWS, TXT_ROWS), TXT_ROWS)
    take(trecv.at[pl.ds(1, NX - 1)], once_recv.at[1])
    trecv[0] = tsend[...]
    for h in range(HEADS):
        parts = [trecv[k, h, :TXT_ROWS].astype(F32) for k in range(NX)]
        levels = [to_column(trecv[k, h, TXT_ROWS:].astype(F32), TXT_ROWS) for k in range(NX)]
        tout[mine, h * HEAD_DIM:(h + 1) * HEAD_DIM] = merge(parts, levels)
    for k in range(1, 2 * NZ):
        remote(tout.at[mine], tout.at[mine], send_sem.at[6], once_recv.at[5], text_device(k)).start()

    take(yrecv.at[pl.ds(2, 5)], once_recv.at[4])
    for k in (1, 2, 4, 6, 7):
        total = total + yrecv[PLACE[k]].astype(F32)
    out[...] = total.astype(BF16)

    rest = tout.at[pl.ds(0, (2 * NZ - 1) * TXT_ROWS)]
    take(rest, once_recv.at[5])
    for index, ref in enumerate((kv.at[:, pl.ds(0, 7), 0], kv.at[:, :, 0],
                                 q.at[pl.ds(GROUP[1], 3 * ROWS)], osend,
                                 trecv.at[pl.ds(1, NX - 1)], ysend, rest)):
        take(ref, send_sem.at[index])


def local(video_q, video_k, video_v, text_q, text_k, text_v, tile_mask, out_weight):
    hbm = pl.BlockSpec(memory_space=pltpu.HBM)
    vmem = pl.BlockSpec(memory_space=pltpu.VMEM)
    dma = pltpu.SemaphoreType.DMA
    in_hbm = functools.partial(pltpu.with_memory_space_constraint, memory_space=pltpu.HBM)
    regular = pltpu.SemaphoreType.REGULAR
    return pl.pallas_call(
        body,
        out_shape=(
            jax.ShapeDtypeStruct((ROWS, FEATURES), BF16),
            jax.ShapeDtypeStruct((2 * NZ * TXT_ROWS, FEATURES), BF16),
        ),
        in_specs=[hbm] * 6 + [hbm, hbm],
        out_specs=(vmem, vmem),
        scratch_shapes=[
            pltpu.VMEM((QUERIES, FEATURES), BF16),
            pltpu.VMEM((HEADS, NZ, 2, 2, ROWS, HEAD_DIM), BF16),
            pltpu.VMEM((2, HEAD_DIM, FEATURES), BF16),
            pltpu.VMEM((5, QUERIES, STEP_KEYS), F32),
            pltpu.VMEM((HEADS, QUERIES, 2 * HEAD_DIM), F32),
            pltpu.VMEM((HEADS, QUERIES, HEAD_DIM), F32),
            pltpu.VMEM((HEADS, NX - 1, ROWS + 16, HEAD_DIM), BF16),
            pltpu.VMEM((HEADS, NX - 1, ROWS + 16, HEAD_DIM), BF16),
            pltpu.VMEM((HEADS, TXT_ROWS + 16, HEAD_DIM), BF16),
            pltpu.VMEM((NX, HEADS, TXT_ROWS + 16, HEAD_DIM), BF16),
            pltpu.VMEM((ROWS, FEATURES), BF16),
            pltpu.VMEM((NY, FEATURES, FEATURES), BF16),
            pltpu.VMEM((NY - 1, ROWS, FEATURES), BF16),
            pltpu.VMEM((NY - 1, ROWS, FEATURES), BF16),
            pltpu.VMEM((ROWS, FEATURES), F32),
            pltpu.SMEM((TILES, TILES), jnp.int32),
            dma((6,)),
            dma((7,)),
            dma((HEADS, 2, 4)),
            dma((HEADS, 5)),
            dma((HEADS, NX - 1)),
            dma((6,)),
            regular((3,)), regular((3,)),
        ],
        compiler_params=pltpu.CompilerParams(
            collective_id=0, has_side_effects=True, vmem_limit_bytes=40 * 2**20),
    )(*map(in_hbm, (video_q, video_k, video_v, text_q, text_k, text_v, tile_mask, out_weight)))


def solution(mesh):
    placed = (
        P("ctx", "head"),
        P("ctx", "head"),
        P("ctx", "head"),
        P(None, "head"),
        P(None, "head"),
        P(None, "head"),
        P(),
        P("head", None),
    )
    return jax.shard_map(
        local,
        mesh=mesh,
        in_specs=placed,
        out_specs=(P("ctx", "head"), P(None, "head")),
        check_vma=False,
    )
```

```python
import functools
import math

import jax
import jax.numpy as jnp
from jax import lax
from jax.experimental import pallas as pl
from jax.experimental.pallas import tpu as pltpu
from jax.sharding import PartitionSpec as P

HEAD_DIM = 128
ROWS = 64
HEADS = 3
NZ, NX, NY = 8, 4, 8
FEATURES = HEADS * HEAD_DIM
TXT_ROWS = 16
TXT_KEYS = 64
TEXT = 64
GROUP = {0: 0, 1: 80, 3: 144, 2: 208}
FAR = 272
QUERIES = 288
USED = (288, 272, 208, 208, 64)
STEP_KEYS = 256
TILES = NZ * NX
PLACE = {3: 0, 5: 1, 4: 2, 1: 3, 2: 4, 6: 5, 7: 6}
NEG = -1e30
SCALE = math.log2(math.e) / math.sqrt(HEAD_DIM)
MESH = pl.DeviceIdType.MESH
BF16, F32 = jnp.bfloat16, jnp.float32


def body(vq, vk, vv, tq, tk, tv, mask, w, out, tout,
         q, kv, tkv, bias, acc, top, osend, orecv, tsend, trecv, fsend, frecv, attn, wbuf, ysend, yrecv, yterm,
         reach, load_sem, send_sem, z_recv, s_recv, o_recv, once_recv, relay_recv, up_sem, down_sem):
    ctx, y = lax.axis_index("ctx"), lax.axis_index("head")
    core, x, z = ctx % 2, (ctx // 2) % NX, ctx // (2 * NX)
    row_id = 2 * z + core

    def device(zz, xx, cc, yy):
        return ((zz * NX + xx) * 2 + cc, yy)

    up = device((z + 1) % NZ, x, core, y)
    down = device((z + NZ - 1) % NZ, x, core, y)
    sibling = device(z, x, 1 - core, y)

    def x_device(k):
        return device(z, (x + k) % NX, core, y)

    def y_device(k):
        return (ctx, (y + k) % NY)

    def signal(sem, to):
        pl.semaphore_signal(sem, inc=1, device_id=to, device_id_type=MESH)

    barrier = pltpu.get_barrier_semaphore()
    peers = [up, down, sibling] + [x_device(k) for k in range(1, NX)]
    peers += [y_device(1), y_device(NY - 1)]
    for peer in peers:
        signal(barrier, peer)

    def load(src, dst, sem):
        pltpu.make_async_copy(src, dst, load_sem.at[sem]).start()

    def take(ref, sem):
        pltpu.make_async_copy(ref, ref, sem).wait()

    def remote(src, dst, send, recv, to):
        return pltpu.make_async_remote_copy(
            src_ref=src, dst_ref=dst, send_sem=send, recv_sem=recv,
            device_id=to, device_id_type=MESH)

    def slot(direction, d):
        return {0: 0, 4: 1}.get(d, 2 * d + direction)

    def z_copy(h, part, direction, d):
        src = kv.at[h, slot(direction, d - 1), core]
        dst = kv.at[h, slot(direction, d), core]
        if part is not None:
            src, dst = src.at[part], dst.at[part]
        if d == 1:
            src = (vk, vv)[part].at[:, pl.ds(h * HEAD_DIM, HEAD_DIM)]
        return remote(src, dst, send_sem.at[0], z_recv.at[h, direction, d - 1],
                      up if direction == 0 else down)

    def s_copy(h, place, step):
        ref = kv.at[h, place, core]
        return remote(ref, ref, send_sem.at[1], s_recv.at[h, step], sibling)

    def s_own(h, part):
        return remote((vk, vv)[part].at[:, pl.ds(h * HEAD_DIM, HEAD_DIM)], kv.at[h, 0, core, part],
                      send_sem.at[1], s_recv.at[h, 0], sibling)

    def q_copy(k):
        return remote(vq, q.at[pl.ds(GROUP[NX - k], ROWS)], send_sem.at[2], once_recv.at[0],
                      x_device(k))

    pl.semaphore_wait(barrier, len(peers))
    for h in range(HEADS):
        for direction in range(2):
            z_copy(h, 0, direction, 1).start()
            z_copy(h, 1, direction, 1).start()
    for k in (2, 1, 3):
        q_copy(k).start()
    for h in range(HEADS):
        for part in range(2):
            s_own(h, part).start()
    load(mask, reach, 0)
    for h in range(HEADS):
        for part, ref in enumerate((vk, vv)):
            load(ref.at[:, pl.ds(h * HEAD_DIM, HEAD_DIM)], kv.at[h, 0, core, part], 1)
    load(vq, q.at[pl.ds(GROUP[0], ROWS)], 2)
    load(tq.at[pl.ds(row_id * TXT_ROWS, TXT_ROWS)], q.at[pl.ds(TEXT, TXT_ROWS)], 3)
    far_id = (row_id + NZ) % (2 * NZ)
    load(tq.at[pl.ds(far_id * TXT_ROWS, TXT_ROWS)], q.at[pl.ds(FAR, TXT_ROWS)], 6)
    for part, ref in enumerate((tk, tv)):
        load(ref.at[pl.ds(x * TXT_KEYS, TXT_KEYS)], tkv.at[part, pl.ds(0, TXT_KEYS)], 4)
    signal(up_sem.at[0], y_device(1))
    signal(down_sem.at[0], y_device(NY - 1))
    signal(up_sem.at[3], up)
    signal(down_sem.at[3], down)
    for k in range(NY):
        load(w.at[:, pl.ds(((y + k) % NY) * FEATURES, FEATURES)], wbuf.at[k], 5)
    take(reach, load_sem.at[0])

    for s in range(5):
        for half in range(2):
            cols = slice(half * HEAD_DIM, (half + 1) * HEAD_DIM)
            if half == 1 and s == 4:
                continue
            if half == 1 and s == 0:
                lane = lax.broadcasted_iota(jnp.int32, (QUERIES, HEAD_DIM), 1)
                row = lax.broadcasted_iota(jnp.int32, (QUERIES, HEAD_DIM), 0)
                bias[0, :, cols] = jnp.where((lane < TXT_KEYS) & (row < FAR), 0.0, NEG).astype(F32)
                continue
            tile_z = (z + NZ - s) % NZ if half == 0 else (z + s) % NZ
            for k in range(NX):
                if GROUP[k] >= USED[s]:
                    continue
                allowed = reach[z * NX + (x + k) % NX, tile_z * NX + x].astype(F32)
                bias[s, GROUP[k]:GROUP[k] + ROWS, cols] = jnp.full(
                    (ROWS, HEAD_DIM), (1.0 - allowed) * NEG, F32)
            for first in (TEXT, FAR):
                if first < USED[s]:
                    bias[s, first:first + TXT_ROWS, cols] = jnp.zeros((TXT_ROWS, HEAD_DIM), F32)
    for part in range(2):
        tkv[part, TXT_KEYS:] = jnp.zeros((HEAD_DIM - TXT_KEYS, FEATURES), BF16)

    def pass_on(sem):
        pl.semaphore_wait(up_sem.at[sem - 1], 1)
        pl.semaphore_wait(down_sem.at[sem - 1], 1)
        signal(up_sem.at[sem], up)
        signal(down_sem.at[sem], down)

    pass_on(4)
    ones = jnp.ones((STEP_KEYS, HEAD_DIM), BF16)

    def absorb(h, s):
        cols = slice(h * HEAD_DIM, (h + 1) * HEAD_DIM)
        slots = {0: (0,), 4: (1,)}.get(s, (2 * s, 2 * s + 1))
        used = USED[s]
        keys = [kv[h, slot, cc, 0] for slot in slots for cc in range(2)]
        values = [kv[h, slot, cc, 1] for slot in slots for cc in range(2)]
        if s == 0:
            keys.append(tkv[0, :, cols])
            values.append(tkv[1, :, cols])
        keys, values = jnp.concatenate(keys, 0), jnp.concatenate(values, 0)
        count = keys.shape[0]
        scores = lax.dot_general(q[:used, cols], keys, (((1,), (1,)), ((), ())),
                                 preferred_element_type=F32)
        scores = scores * SCALE + bias[s, :used, :count]
        high = jnp.max(scores, axis=1, keepdims=True)
        if s:
            before = top[h, :used][:, :1]
            high = jnp.maximum(high, before)
        weights = jnp.exp2(scores - high).astype(BF16)
        values = jnp.concatenate([values, ones[:count]], 1)
        summed = jnp.dot(weights, values, preferred_element_type=F32)
        if s:
            summed = summed + acc[h, :used] * jnp.exp2(before - high)
        acc[h, :used] = summed
        top[h, :used] = jnp.broadcast_to(high, (used, HEAD_DIM))

    def forward(h, d):
        for direction in range(2):
            if d < 4:
                ref = kv.at[h, slot(direction, d), core]
            else:
                ref = kv.at[h, 1, core, direction]
            take(ref, z_recv.at[h, direction, d - 1])
            if d < 4:
                z_copy(h, direction if d == 3 else None, direction, d + 1).start()
        for place in (slot(0, d), slot(1, d)) if d < 4 else (1,):
            s_copy(h, place, d).start()

    def from_sibling(h, s):
        places = {0: 0, 4: 1}.get(s, pl.ds(2 * s, 2))
        take(kv.at[h, places, 1 - core], s_recv.at[h, s])

    def eye(rows):
        return (lax.broadcasted_iota(jnp.int32, (rows, HEAD_DIM), 0)
                == lax.broadcasted_iota(jnp.int32, (rows, HEAD_DIM), 1))

    def finish(h, first, rows):
        block = slice(first, first + rows)
        total = acc[h, block, HEAD_DIM:]
        return acc[h, block, :HEAD_DIM] / total, top[h, block] + jnp.log2(total)

    def to_rows(level):
        row = jnp.sum(jnp.where(eye(level.shape[0]), level, 0.0), axis=0, keepdims=True)
        first = row.astype(BF16).astype(F32)
        second = (row - first).astype(BF16).astype(F32)
        index = lax.broadcasted_iota(jnp.int32, (16, HEAD_DIM), 0)
        rest = jnp.where(index == 1, second, jnp.where(index == 2, row - first - second, 0.0))
        return jnp.where(index == 0, first, rest).astype(BF16)

    def to_column(rows, count):
        row = rows[0:1] + rows[1:2] + rows[2:3]
        return jnp.sum(jnp.where(eye(count), jnp.broadcast_to(row, (count, HEAD_DIM)), 0.0),
                       axis=1, keepdims=True)

    def o_copy(h, k):
        return remote(osend.at[h, k - 1], orecv.at[h, k - 1], send_sem.at[3], o_recv.at[h, k - 1],
                      x_device(k))

    def give(h, k):
        block, level = finish(h, GROUP[k], ROWS)
        osend[h, k - 1, :ROWS] = block.astype(BF16)
        osend[h, k - 1, ROWS:] = to_rows(level)
        o_copy(h, k).start()

    def fold(h, first, rows, sources):
        block = slice(first, first + rows)
        before = top[h, block][:, :1]
        parts, levels = [acc[h, block]], [before]
        for source in sources:
            part = source[:rows].astype(F32)
            parts.append(jnp.concatenate([part, jnp.ones((rows, HEAD_DIM), F32)], 1))
            levels.append(to_column(source[rows:].astype(F32), rows))
        high = functools.reduce(jnp.maximum, levels)
        acc[h, block] = functools.reduce(
            jnp.add, [part * jnp.exp2(level - high) for part, level in zip(parts, levels)])
        top[h, block] = jnp.broadcast_to(high, (rows, HEAD_DIM))

    def pack_text(h, first, to):
        part, level = finish(h, first, TXT_ROWS)
        to[h, :TXT_ROWS] = part.astype(BF16)
        to[h, TXT_ROWS:] = to_rows(level)

    def merge(parts, levels):
        high = functools.reduce(jnp.maximum, levels)
        shares = [jnp.exp2(level - high) for level in levels]
        total = functools.reduce(jnp.add, shares)
        return functools.reduce(
            jnp.add, [part * (share / total) for part, share in zip(parts, shares)]).astype(BF16)

    for h in range(HEADS):
        forward(h, 1)
    pass_on(5)
    take(kv.at[:, 0, core], load_sem.at[1])
    take(q.at[pl.ds(GROUP[0], ROWS)], load_sem.at[2])
    take(q.at[pl.ds(TEXT, TXT_ROWS)], load_sem.at[3])
    take(q.at[pl.ds(FAR, TXT_ROWS)], load_sem.at[6])
    take(tkv.at[:, pl.ds(0, TXT_KEYS)], load_sem.at[4])
    take(q.at[pl.ds(GROUP[1], 3 * ROWS)], once_recv.at[0])
    for h in range(HEADS):
        from_sibling(h, 0)
        absorb(h, 0)
    for h in range(HEADS):
        pack_text(h, FAR, fsend)
    pl.semaphore_wait(up_sem.at[5], 1)
    pl.semaphore_wait(down_sem.at[5], 1)
    remote(fsend, frecv, send_sem.at[7], once_recv.at[6], device((z + 4) % NZ, x, core, y)).start()
    for h in range(HEADS):
        forward(h, 2)
        from_sibling(h, 1)
        absorb(h, 1)
        give(h, 2)
    pl.semaphore_wait(up_sem.at[0], 1)
    pl.semaphore_wait(down_sem.at[0], 1)
    signal(up_sem.at[1], y_device(1))
    signal(down_sem.at[1], y_device(NY - 1))
    for h in range(HEADS):
        forward(h, 3)
        from_sibling(h, 2)
        absorb(h, 2)
    pl.semaphore_wait(up_sem.at[1], 1)
    pl.semaphore_wait(down_sem.at[1], 1)
    signal(up_sem.at[2], y_device(1))
    signal(down_sem.at[2], y_device(NY - 1))
    for h in range(HEADS):
        from_sibling(h, 3)
        absorb(h, 3)
        give(h, 1)
        give(h, 3)

    def x_copy(k):
        return remote(tsend, trecv.at[k], send_sem.at[4], once_recv.at[1], x_device(k))

    take(frecv, once_recv.at[6])
    for h in range(HEADS):
        fold(h, TEXT, TXT_ROWS, [frecv.at[h]])
    for h in range(HEADS):
        pack_text(h, TEXT, tsend)
    for k in (2, 1, 3):
        x_copy(k).start()
    for h in range(HEADS):
        forward(h, 4)
    pl.semaphore_wait(up_sem.at[2], 1)
    pl.semaphore_wait(down_sem.at[2], 1)
    take(wbuf, load_sem.at[5])

    for h in range(HEADS):
        for k in range(1, NX):
            o_copy(h, k).wait_recv()
    for h in range(HEADS):
        fold(h, GROUP[0], ROWS, [orecv.at[h, k - 1] for k in range(1, NX)])
    for h in range(HEADS):
        from_sibling(h, 4)
    for h in range(HEADS):
        absorb(h, 4)
    own = slice(GROUP[0], GROUP[0] + ROWS)
    for h in range(HEADS):
        attn[:, h * HEAD_DIM:(h + 1) * HEAD_DIM] = (
            acc[h, own, :HEAD_DIM] / acc[h, own, HEAD_DIM:]).astype(BF16)

    def product(k):
        return jnp.dot(attn[...], wbuf[k], preferred_element_type=F32)

    halves = (slice(0, ROWS // 2), slice(ROWS // 2, ROWS))

    def y_copy(k, half=None, way=0):
        to = {3: 1, 5: NY - 1, 4: (2, NY - 2)[way]}.get(k, k)
        src, dst, sem = ysend.at[PLACE[k]], yrecv.at[PLACE[k]], once_recv.at[4]
        if half is not None:
            rows = pl.ds(half * (ROWS // 2), ROWS // 2)
            src, dst = src.at[rows], dst.at[rows]
        if k in (3, 4, 5):
            sem = relay_recv.at[PLACE[k], half]
        return remote(src, dst, send_sem.at[5], sem, y_device(to))

    ysend[PLACE[4]] = product(4).astype(BF16)
    for half in range(2):
        y_copy(4, half, half).start()
    for k in (3, 5):
        ysend[PLACE[k]] = product(k).astype(BF16)
    for first in range(2):
        y_copy(3, 1 - first).start()
        y_copy(5, first).start()

    mine = tout.at[row_id]
    take(trecv.at[pl.ds(1, NX - 1)], once_recv.at[1])
    trecv[0] = tsend[...]
    for h in range(HEADS):
        parts = [trecv[k, h, :TXT_ROWS].astype(F32) for k in range(NX)]
        levels = [to_column(trecv[k, h, TXT_ROWS:].astype(F32), TXT_ROWS) for k in range(NX)]
        mine[:, h * HEAD_DIM:(h + 1) * HEAD_DIM] = merge(parts, levels)
    for k in (8, 9, 7, 10, 6, 11, 5, 12, 4, 13, 3, 14, 2, 15, 1):
        other = (row_id + k) % (2 * NZ)
        to = device(other // 2, x, other % 2, y)
        remote(mine, mine, send_sem.at[6], once_recv.at[5], to).start()

    for way, k in enumerate((2, 6)):
        yterm[way] = product(k)
    for step in range(2):
        for way, (k, relay) in enumerate(((2, 3), (6, 5))):
            half = way if step else 1 - way
            rows = halves[half]
            y_copy(relay, half).wait_recv()
            yterm[way, rows] += yrecv[PLACE[relay], rows].astype(F32)
            if step:
                y_copy(4, half, way).wait_recv()
                yterm[way, rows] += yrecv[PLACE[4], rows].astype(F32)
            ysend[PLACE[k], rows] = yterm[way, rows].astype(BF16)
            y_copy(k, half).start()
    for k in (1, 7):
        ysend[PLACE[k]] = product(k).astype(BF16)
        y_copy(k).start()
    total = product(0)

    take(yrecv.at[pl.ds(3, 4)], once_recv.at[4])
    for k in (1, 2, 6, 7):
        total = total + yrecv[PLACE[k]].astype(F32)
    out[...] = total.astype(BF16)

    others = tout.at[pl.ds(0, 2 * NZ - 1)]
    take(others, once_recv.at[5])
    for index, ref in enumerate((kv.at[:, pl.ds(0, 7), 0], kv.at[:, :, 0],
                                 q.at[pl.ds(GROUP[1], 3 * ROWS)], osend,
                                 trecv.at[pl.ds(1, NX - 1)], ysend, others, fsend)):
        take(ref, send_sem.at[index])


def local(video_q, video_k, video_v, text_q, text_k, text_v, tile_mask, out_weight):
    hbm = pl.BlockSpec(memory_space=pltpu.HBM)
    vmem = pl.BlockSpec(memory_space=pltpu.VMEM)
    dma = pltpu.SemaphoreType.DMA
    in_hbm = functools.partial(pltpu.with_memory_space_constraint, memory_space=pltpu.HBM)
    regular = pltpu.SemaphoreType.REGULAR
    video, text = pl.pallas_call(
        body,
        out_shape=(
            jax.ShapeDtypeStruct((ROWS, FEATURES), BF16),
            jax.ShapeDtypeStruct((2 * NZ, TXT_ROWS, FEATURES), BF16),
        ),
        in_specs=[hbm] * 6 + [hbm, hbm],
        out_specs=(vmem, vmem),
        scratch_shapes=[
            pltpu.VMEM((QUERIES, FEATURES), BF16),
            pltpu.VMEM((HEADS, NZ, 2, 2, ROWS, HEAD_DIM), BF16),
            pltpu.VMEM((2, HEAD_DIM, FEATURES), BF16),
            pltpu.VMEM((5, QUERIES, STEP_KEYS), F32),
            pltpu.VMEM((HEADS, QUERIES, 2 * HEAD_DIM), F32),
            pltpu.VMEM((HEADS, QUERIES, HEAD_DIM), F32),
            pltpu.VMEM((HEADS, NX - 1, ROWS + 16, HEAD_DIM), BF16),
            pltpu.VMEM((HEADS, NX - 1, ROWS + 16, HEAD_DIM), BF16),
            pltpu.VMEM((HEADS, TXT_ROWS + 16, HEAD_DIM), BF16),
            pltpu.VMEM((NX, HEADS, TXT_ROWS + 16, HEAD_DIM), BF16),
            pltpu.VMEM((HEADS, TXT_ROWS + 16, HEAD_DIM), BF16),
            pltpu.VMEM((HEADS, TXT_ROWS + 16, HEAD_DIM), BF16),
            pltpu.VMEM((ROWS, FEATURES), BF16),
            pltpu.VMEM((NY, FEATURES, FEATURES), BF16),
            pltpu.VMEM((NY - 1, ROWS, FEATURES), BF16),
            pltpu.VMEM((NY - 1, ROWS, FEATURES), BF16),
            pltpu.VMEM((2, ROWS, FEATURES), F32),
            pltpu.SMEM((TILES, TILES), jnp.int32),
            dma((7,)),
            dma((8,)),
            dma((HEADS, 2, 4)),
            dma((HEADS, 5)),
            dma((HEADS, NX - 1)),
            dma((7,)),
            dma((3, 2)),
            regular((6,)), regular((6,)),
        ],
        compiler_params=pltpu.CompilerParams(
            collective_id=0, has_side_effects=True, vmem_limit_bytes=40 * 2**20),
    )(*map(in_hbm, (video_q, video_k, video_v, text_q, text_k, text_v, tile_mask, out_weight)))
    return video, text.reshape(2 * NZ * TXT_ROWS, FEATURES)


def solution(mesh):
    placed = (
        P("ctx", "head"),
        P("ctx", "head"),
        P("ctx", "head"),
        P(None, "head"),
        P(None, "head"),
        P(None, "head"),
        P(),
        P("head", None),
    )
    return jax.shard_map(
        local,
        mesh=mesh,
        in_specs=placed,
        out_specs=(P("ctx", "head"), P(None, "head")),
        check_vma=False,
    )
```

```python
import functools
import math

import jax
import jax.numpy as jnp
from jax import lax
from jax.experimental import pallas as pl
from jax.experimental.pallas import tpu as pltpu
from jax.sharding import PartitionSpec as P

HEAD_DIM = 128
ROWS = 64
HEADS = 3
NZ, NX, NY = 8, 4, 8
FEATURES = HEADS * HEAD_DIM
TXT_ROWS = 16
TXT_KEYS = 64
TEXT = 64
GROUP = {0: 0, 1: 80, 3: 144, 2: 208}
FAR = 272
QUERIES = 288
USED = (288, 272, 208, 208, 64)
STEP_KEYS = 256
TILES = NZ * NX
PLACE = {3: 0, 5: 1, 4: 2, 1: 3, 2: 4, 6: 5, 7: 6}
NEG = -1e30
SCALE = math.log2(math.e) / math.sqrt(HEAD_DIM)
MESH = pl.DeviceIdType.MESH
BF16, F32 = jnp.bfloat16, jnp.float32


def body(vq, vk, vv, tq, tk, tv, mask, w, out, tout,
         q, kv, tkv, bias, acc, top, osend, orecv, tsend, trecv, fsend, frecv, attn, wbuf, ysend, yrecv, yterm,
         reach, load_sem, send_sem, z_recv, s_recv, o_recv, once_recv, relay_recv, up_sem, down_sem):
    ctx, y = lax.axis_index("ctx"), lax.axis_index("head")
    core, x, z = ctx % 2, (ctx // 2) % NX, ctx // (2 * NX)
    row_id = 2 * z + core

    def device(zz, xx, cc, yy):
        return ((zz * NX + xx) * 2 + cc, yy)

    up = device((z + 1) % NZ, x, core, y)
    down = device((z + NZ - 1) % NZ, x, core, y)
    sibling = device(z, x, 1 - core, y)

    def x_device(k):
        return device(z, (x + k) % NX, core, y)

    def y_device(k):
        return (ctx, (y + k) % NY)

    def signal(sem, to):
        pl.semaphore_signal(sem, inc=1, device_id=to, device_id_type=MESH)

    barrier = pltpu.get_barrier_semaphore()
    peers = [up, down, sibling] + [x_device(k) for k in range(1, NX)]
    peers += [y_device(1), y_device(NY - 1)]
    for peer in peers:
        signal(barrier, peer)

    def load(src, dst, sem):
        pltpu.make_async_copy(src, dst, load_sem.at[sem]).start()

    def take(ref, sem):
        pltpu.make_async_copy(ref, ref, sem).wait()

    def remote(src, dst, send, recv, to):
        return pltpu.make_async_remote_copy(
            src_ref=src, dst_ref=dst, send_sem=send, recv_sem=recv,
            device_id=to, device_id_type=MESH)

    def slot(direction, d):
        return {0: 0, 4: 1}.get(d, 2 * d + direction)

    def z_copy(h, part, direction, d):
        src = kv.at[h, slot(direction, d - 1), core]
        dst = kv.at[h, slot(direction, d), core]
        if part is not None:
            src, dst = src.at[part], dst.at[part]
        if d == 1:
            src = (vk, vv)[part].at[:, pl.ds(h * HEAD_DIM, HEAD_DIM)]
        return remote(src, dst, send_sem.at[0], z_recv.at[h, direction, d - 1],
                      up if direction == 0 else down)

    def s_copy(h, place, step):
        ref = kv.at[h, place, core]
        return remote(ref, ref, send_sem.at[1], s_recv.at[h, step], sibling)

    def s_own(h, part):
        return remote((vk, vv)[part].at[:, pl.ds(h * HEAD_DIM, HEAD_DIM)], kv.at[h, 0, core, part],
                      send_sem.at[1], s_recv.at[h, 0], sibling)

    def q_copy(k):
        return remote(vq, q.at[pl.ds(GROUP[NX - k], ROWS)], send_sem.at[2], once_recv.at[0],
                      x_device(k))

    pl.semaphore_wait(barrier, len(peers))
    for h in range(HEADS):
        for direction in range(2):
            for part in range(2):
                z_copy(h, part, direction, 1).start()
        for part in range(2):
            s_own(h, part).start()
    for k in (2, 1, 3):
        q_copy(k).start()
    load(mask, reach, 0)
    for h in range(HEADS):
        for part, ref in enumerate((vk, vv)):
            load(ref.at[:, pl.ds(h * HEAD_DIM, HEAD_DIM)], kv.at[h, 0, core, part], 1)
    load(vq, q.at[pl.ds(GROUP[0], ROWS)], 2)
    load(tq.at[pl.ds(row_id * TXT_ROWS, TXT_ROWS)], q.at[pl.ds(TEXT, TXT_ROWS)], 3)
    far_id = (row_id + NZ) % (2 * NZ)
    load(tq.at[pl.ds(far_id * TXT_ROWS, TXT_ROWS)], q.at[pl.ds(FAR, TXT_ROWS)], 6)
    for part, ref in enumerate((tk, tv)):
        load(ref.at[pl.ds(x * TXT_KEYS, TXT_KEYS)], tkv.at[part, pl.ds(0, TXT_KEYS)], 4)
    signal(up_sem.at[0], y_device(1))
    signal(down_sem.at[0], y_device(NY - 1))
    signal(up_sem.at[3], up)
    signal(down_sem.at[3], down)
    for k in range(NY):
        load(w.at[:, pl.ds(((y + k) % NY) * FEATURES, FEATURES)], wbuf.at[k], 5)
    take(reach, load_sem.at[0])

    for s in range(5):
        for half in range(2):
            cols = slice(half * HEAD_DIM, (half + 1) * HEAD_DIM)
            if half == 1 and s == 4:
                continue
            if half == 1 and s == 0:
                lane = lax.broadcasted_iota(jnp.int32, (QUERIES, HEAD_DIM), 1)
                row = lax.broadcasted_iota(jnp.int32, (QUERIES, HEAD_DIM), 0)
                bias[0, :, cols] = jnp.where((lane < TXT_KEYS) & (row < FAR), 0.0, NEG).astype(F32)
                continue
            tile_z = (z + NZ - s) % NZ if half == 0 else (z + s) % NZ
            for k in range(NX):
                if GROUP[k] >= USED[s]:
                    continue
                allowed = reach[z * NX + (x + k) % NX, tile_z * NX + x].astype(F32)
                bias[s, GROUP[k]:GROUP[k] + ROWS, cols] = jnp.full(
                    (ROWS, HEAD_DIM), (1.0 - allowed) * NEG, F32)
            for first in (TEXT, FAR):
                if first < USED[s]:
                    bias[s, first:first + TXT_ROWS, cols] = jnp.zeros((TXT_ROWS, HEAD_DIM), F32)
    for part in range(2):
        tkv[part, TXT_KEYS:] = jnp.zeros((HEAD_DIM - TXT_KEYS, FEATURES), BF16)

    def pass_on(sem):
        pl.semaphore_wait(up_sem.at[sem - 1], 1)
        pl.semaphore_wait(down_sem.at[sem - 1], 1)
        signal(up_sem.at[sem], up)
        signal(down_sem.at[sem], down)

    pass_on(4)
    ones = jnp.ones((STEP_KEYS, HEAD_DIM), BF16)

    def absorb(h, s):
        cols = slice(h * HEAD_DIM, (h + 1) * HEAD_DIM)
        slots = {0: (0,), 4: (1,)}.get(s, (2 * s, 2 * s + 1))
        used = USED[s]
        keys = [kv[h, slot, cc, 0] for slot in slots for cc in range(2)]
        values = [kv[h, slot, cc, 1] for slot in slots for cc in range(2)]
        if s == 0:
            keys.append(tkv[0, :, cols])
            values.append(tkv[1, :, cols])
        keys, values = jnp.concatenate(keys, 0), jnp.concatenate(values, 0)
        count = keys.shape[0]
        scores = lax.dot_general(q[:used, cols], keys, (((1,), (1,)), ((), ())),
                                 preferred_element_type=F32)
        scores = scores * SCALE + bias[s, :used, :count]
        high = jnp.max(scores, axis=1, keepdims=True)
        if s:
            before = top[h, :used][:, :1]
            high = jnp.maximum(high, before)
        weights = jnp.exp2(scores - high).astype(BF16)
        values = jnp.concatenate([values, ones[:count]], 1)
        summed = jnp.dot(weights, values, preferred_element_type=F32)
        if s:
            summed = summed + acc[h, :used] * jnp.exp2(before - high)
        acc[h, :used] = summed
        top[h, :used] = jnp.broadcast_to(high, (used, HEAD_DIM))

    def forward(h, d):
        for direction in range(2):
            if d < 4:
                ref = kv.at[h, slot(direction, d), core]
            else:
                ref = kv.at[h, 1, core, direction]
            take(ref, z_recv.at[h, direction, d - 1])
            if d < 4:
                z_copy(h, direction if d == 3 else None, direction, d + 1).start()
        s_copy(h, pl.ds(2 * d, 2) if d < 4 else 1, d).start()

    def from_sibling(h, s):
        places = {0: 0, 4: 1}.get(s, pl.ds(2 * s, 2))
        take(kv.at[h, places, 1 - core], s_recv.at[h, s])

    def eye(rows):
        return (lax.broadcasted_iota(jnp.int32, (rows, HEAD_DIM), 0)
                == lax.broadcasted_iota(jnp.int32, (rows, HEAD_DIM), 1))

    def finish(h, first, rows):
        block = slice(first, first + rows)
        total = acc[h, block, HEAD_DIM:]
        return acc[h, block, :HEAD_DIM] / total, top[h, block] + jnp.log2(total)

    def to_rows(level):
        row = jnp.sum(jnp.where(eye(level.shape[0]), level, 0.0), axis=0, keepdims=True)
        first = row.astype(BF16).astype(F32)
        second = (row - first).astype(BF16).astype(F32)
        index = lax.broadcasted_iota(jnp.int32, (16, HEAD_DIM), 0)
        rest = jnp.where(index == 1, second, jnp.where(index == 2, row - first - second, 0.0))
        return jnp.where(index == 0, first, rest).astype(BF16)

    def to_column(rows, count):
        row = rows[0:1] + rows[1:2] + rows[2:3]
        return jnp.sum(jnp.where(eye(count), jnp.broadcast_to(row, (count, HEAD_DIM)), 0.0),
                       axis=1, keepdims=True)

    def o_copy(h, k):
        return remote(osend.at[h, k - 1], orecv.at[h, k - 1], send_sem.at[3], o_recv.at[h, k - 1],
                      x_device(k))

    def give(h, k):
        block, level = finish(h, GROUP[k], ROWS)
        osend[h, k - 1, :ROWS] = block.astype(BF16)
        osend[h, k - 1, ROWS:] = to_rows(level)
        o_copy(h, k).start()

    def fold(h, first, rows, sources):
        block = slice(first, first + rows)
        before = top[h, block][:, :1]
        parts, levels = [acc[h, block]], [before]
        for source in sources:
            part = source[:rows].astype(F32)
            parts.append(jnp.concatenate([part, jnp.ones((rows, HEAD_DIM), F32)], 1))
            levels.append(to_column(source[rows:].astype(F32), rows))
        high = functools.reduce(jnp.maximum, levels)
        acc[h, block] = functools.reduce(
            jnp.add, [part * jnp.exp2(level - high) for part, level in zip(parts, levels)])
        top[h, block] = jnp.broadcast_to(high, (rows, HEAD_DIM))

    def pack_text(h, first, to):
        part, level = finish(h, first, TXT_ROWS)
        to[h, :TXT_ROWS] = part.astype(BF16)
        to[h, TXT_ROWS:] = to_rows(level)

    def merge(parts, levels):
        high = functools.reduce(jnp.maximum, levels)
        shares = [jnp.exp2(level - high) for level in levels]
        total = functools.reduce(jnp.add, shares)
        return functools.reduce(
            jnp.add, [part * (share / total) for part, share in zip(parts, shares)]).astype(BF16)

    for h in range(HEADS):
        forward(h, 1)
    pass_on(5)
    take(kv.at[:, 0, core], load_sem.at[1])
    take(q.at[pl.ds(GROUP[0], ROWS)], load_sem.at[2])
    take(q.at[pl.ds(TEXT, TXT_ROWS)], load_sem.at[3])
    take(q.at[pl.ds(FAR, TXT_ROWS)], load_sem.at[6])
    take(tkv.at[:, pl.ds(0, TXT_KEYS)], load_sem.at[4])
    take(q.at[pl.ds(GROUP[1], 3 * ROWS)], once_recv.at[0])
    for h in range(HEADS):
        from_sibling(h, 0)
        absorb(h, 0)
    for h in range(HEADS):
        pack_text(h, FAR, fsend)
    pl.semaphore_wait(up_sem.at[5], 1)
    pl.semaphore_wait(down_sem.at[5], 1)
    remote(fsend, frecv, send_sem.at[7], once_recv.at[6], device((z + 4) % NZ, x, core, y)).start()
    for h in range(HEADS):
        forward(h, 2)
        from_sibling(h, 1)
        absorb(h, 1)
        give(h, 2)
    pl.semaphore_wait(up_sem.at[0], 1)
    pl.semaphore_wait(down_sem.at[0], 1)
    signal(up_sem.at[1], y_device(1))
    signal(down_sem.at[1], y_device(NY - 1))
    for h in range(HEADS):
        forward(h, 3)
        from_sibling(h, 2)
        absorb(h, 2)
    pl.semaphore_wait(up_sem.at[1], 1)
    pl.semaphore_wait(down_sem.at[1], 1)
    signal(up_sem.at[2], y_device(1))
    signal(down_sem.at[2], y_device(NY - 1))
    for h in range(HEADS):
        from_sibling(h, 3)
        absorb(h, 3)
        give(h, 1)
        give(h, 3)

    def x_copy(k):
        return remote(tsend, trecv.at[k], send_sem.at[4], once_recv.at[1], x_device(k))

    take(frecv, once_recv.at[6])
    for h in range(HEADS):
        fold(h, TEXT, TXT_ROWS, [frecv.at[h]])
    for h in range(HEADS):
        pack_text(h, TEXT, tsend)
    for k in (2, 1, 3):
        x_copy(k).start()
    for h in range(HEADS):
        forward(h, 4)
    pl.semaphore_wait(up_sem.at[2], 1)
    pl.semaphore_wait(down_sem.at[2], 1)
    take(wbuf, load_sem.at[5])

    for h in range(HEADS):
        for k in range(1, NX):
            o_copy(h, k).wait_recv()
    for h in range(HEADS):
        fold(h, GROUP[0], ROWS, [orecv.at[h, k - 1] for k in range(1, NX)])
    for h in range(HEADS):
        from_sibling(h, 4)
    for h in range(HEADS):
        absorb(h, 4)
    own = slice(GROUP[0], GROUP[0] + ROWS)
    for h in range(HEADS):
        attn[:, h * HEAD_DIM:(h + 1) * HEAD_DIM] = (
            acc[h, own, :HEAD_DIM] / acc[h, own, HEAD_DIM:]).astype(BF16)

    def product(k):
        return jnp.dot(attn[...], wbuf[k], preferred_element_type=F32)

    halves = (slice(0, ROWS // 2), slice(ROWS // 2, ROWS))

    def y_copy(k, half=None, way=0):
        to = {3: 1, 5: NY - 1, 4: (2, NY - 2)[way]}.get(k, k)
        src, dst, sem = ysend.at[PLACE[k]], yrecv.at[PLACE[k]], once_recv.at[4]
        if half is not None:
            rows = pl.ds(half * (ROWS // 2), ROWS // 2)
            src, dst = src.at[rows], dst.at[rows]
        if k in (3, 4, 5):
            sem = relay_recv.at[PLACE[k], half]
        return remote(src, dst, send_sem.at[5], sem, y_device(to))

    ysend[PLACE[4]] = product(4).astype(BF16)
    for half in range(2):
        y_copy(4, half, half).start()
    for k in (3, 5):
        ysend[PLACE[k]] = product(k).astype(BF16)
    for first in range(2):
        y_copy(3, 1 - first).start()
        y_copy(5, first).start()

    mine = tout.at[row_id]
    take(trecv.at[pl.ds(1, NX - 1)], once_recv.at[1])
    trecv[0] = tsend[...]
    for h in range(HEADS):
        parts = [trecv[k, h, :TXT_ROWS].astype(F32) for k in range(NX)]
        levels = [to_column(trecv[k, h, TXT_ROWS:].astype(F32), TXT_ROWS) for k in range(NX)]
        mine[:, h * HEAD_DIM:(h + 1) * HEAD_DIM] = merge(parts, levels)
    for k in range(1, 2 * NZ):
        other = (row_id + k) % (2 * NZ)
        to = device(other // 2, x, other % 2, y)
        remote(mine, mine, send_sem.at[6], once_recv.at[5], to).start()

    for way, k in enumerate((2, 6)):
        yterm[way] = product(k)
    for step in range(2):
        for way, (k, relay) in enumerate(((2, 3), (6, 5))):
            half = way if step else 1 - way
            rows = halves[half]
            y_copy(relay, half).wait_recv()
            yterm[way, rows] += yrecv[PLACE[relay], rows].astype(F32)
            if step:
                y_copy(4, half, way).wait_recv()
                yterm[way, rows] += yrecv[PLACE[4], rows].astype(F32)
            ysend[PLACE[k], rows] = yterm[way, rows].astype(BF16)
            y_copy(k, half).start()
    for k in (1, 7):
        ysend[PLACE[k]] = product(k).astype(BF16)
        y_copy(k).start()
    total = product(0)

    take(yrecv.at[pl.ds(3, 4)], once_recv.at[4])
    for k in (1, 2, 6, 7):
        total = total + yrecv[PLACE[k]].astype(F32)
    out[...] = total.astype(BF16)

    others = tout.at[pl.ds(0, 2 * NZ - 1)]
    take(others, once_recv.at[5])
    for index, ref in enumerate((kv.at[:, pl.ds(0, 7), 0], kv.at[:, :, 0],
                                 q.at[pl.ds(GROUP[1], 3 * ROWS)], osend,
                                 trecv.at[pl.ds(1, NX - 1)], ysend, others, fsend)):
        take(ref, send_sem.at[index])


def local(video_q, video_k, video_v, text_q, text_k, text_v, tile_mask, out_weight):
    hbm = pl.BlockSpec(memory_space=pltpu.HBM)
    vmem = pl.BlockSpec(memory_space=pltpu.VMEM)
    dma = pltpu.SemaphoreType.DMA
    in_hbm = functools.partial(pltpu.with_memory_space_constraint, memory_space=pltpu.HBM)
    regular = pltpu.SemaphoreType.REGULAR
    video, text = pl.pallas_call(
        body,
        out_shape=(
            jax.ShapeDtypeStruct((ROWS, FEATURES), BF16),
            jax.ShapeDtypeStruct((2 * NZ, TXT_ROWS, FEATURES), BF16),
        ),
        in_specs=[hbm] * 6 + [hbm, hbm],
        out_specs=(vmem, vmem),
        scratch_shapes=[
            pltpu.VMEM((QUERIES, FEATURES), BF16),
            pltpu.VMEM((HEADS, NZ, 2, 2, ROWS, HEAD_DIM), BF16),
            pltpu.VMEM((2, HEAD_DIM, FEATURES), BF16),
            pltpu.VMEM((5, QUERIES, STEP_KEYS), F32),
            pltpu.VMEM((HEADS, QUERIES, 2 * HEAD_DIM), F32),
            pltpu.VMEM((HEADS, QUERIES, HEAD_DIM), F32),
            pltpu.VMEM((HEADS, NX - 1, ROWS + 16, HEAD_DIM), BF16),
            pltpu.VMEM((HEADS, NX - 1, ROWS + 16, HEAD_DIM), BF16),
            pltpu.VMEM((HEADS, TXT_ROWS + 16, HEAD_DIM), BF16),
            pltpu.VMEM((NX, HEADS, TXT_ROWS + 16, HEAD_DIM), BF16),
            pltpu.VMEM((HEADS, TXT_ROWS + 16, HEAD_DIM), BF16),
            pltpu.VMEM((HEADS, TXT_ROWS + 16, HEAD_DIM), BF16),
            pltpu.VMEM((ROWS, FEATURES), BF16),
            pltpu.VMEM((NY, FEATURES, FEATURES), BF16),
            pltpu.VMEM((NY - 1, ROWS, FEATURES), BF16),
            pltpu.VMEM((NY - 1, ROWS, FEATURES), BF16),
            pltpu.VMEM((2, ROWS, FEATURES), F32),
            pltpu.SMEM((TILES, TILES), jnp.int32),
            dma((7,)),
            dma((8,)),
            dma((HEADS, 2, 4)),
            dma((HEADS, 5)),
            dma((HEADS, NX - 1)),
            dma((7,)),
            dma((3, 2)),
            regular((6,)), regular((6,)),
        ],
        compiler_params=pltpu.CompilerParams(
            collective_id=0, has_side_effects=True, vmem_limit_bytes=40 * 2**20),
    )(*map(in_hbm, (video_q, video_k, video_v, text_q, text_k, text_v, tile_mask, out_weight)))
    return video, text.reshape(2 * NZ * TXT_ROWS, FEATURES)


def solution(mesh):
    placed = (
        P("ctx", "head"),
        P("ctx", "head"),
        P("ctx", "head"),
        P(None, "head"),
        P(None, "head"),
        P(None, "head"),
        P(),
        P("head", None),
    )
    return jax.shard_map(
        local,
        mesh=mesh,
        in_specs=placed,
        out_specs=(P("ctx", "head"), P(None, "head")),
        check_vma=False,
    )
```

```python
import functools
import math

import jax
import jax.numpy as jnp
from jax import lax
from jax.experimental import pallas as pl
from jax.experimental.pallas import tpu as pltpu
from jax.sharding import PartitionSpec as P

HEAD_DIM = 128
ROWS = 64
HEADS = 3
NZ, NX, NY = 8, 4, 8
FEATURES = HEADS * HEAD_DIM
TXT_ROWS = 16
TXT_KEYS = 64
TEXT = 64
GROUP = {0: 0, 1: 80, 3: 144, 2: 208}
FAR = 272
QUERIES = 288
USED = (288, 272, 208, 208, 64)
STEP_KEYS = 256
TILES = NZ * NX
PLACE = {3: 0, 5: 1, 4: 2, 1: 3, 2: 4, 6: 5, 7: 6}
NEG = -1e30
SCALE = math.log2(math.e) / math.sqrt(HEAD_DIM)
MESH = pl.DeviceIdType.MESH
BF16, F32 = jnp.bfloat16, jnp.float32


def body(vq, vk, vv, tq, tk, tv, mask, w, out, tout,
         q, kv, tkv, bias, acc, top, osend, orecv, tsend, trecv, fsend, frecv, attn, wbuf, ysend, yrecv, yterm,
         reach, load_sem, send_sem, z_recv, s_recv, o_recv, once_recv, relay_recv, up_sem, down_sem):
    ctx, y = lax.axis_index("ctx"), lax.axis_index("head")
    core, x, z = ctx % 2, (ctx // 2) % NX, ctx // (2 * NX)
    row_id = 2 * z + core

    def device(zz, xx, cc, yy):
        return ((zz * NX + xx) * 2 + cc, yy)

    up = device((z + 1) % NZ, x, core, y)
    down = device((z + NZ - 1) % NZ, x, core, y)
    sibling = device(z, x, 1 - core, y)

    def x_device(k):
        return device(z, (x + k) % NX, core, y)

    def y_device(k):
        return (ctx, (y + k) % NY)

    def signal(sem, to):
        pl.semaphore_signal(sem, inc=1, device_id=to, device_id_type=MESH)

    barrier = pltpu.get_barrier_semaphore()
    peers = [up, down, sibling] + [x_device(k) for k in range(1, NX)]
    peers += [y_device(1), y_device(NY - 1)]
    for peer in peers:
        signal(barrier, peer)

    def load(src, dst, sem):
        pltpu.make_async_copy(src, dst, load_sem.at[sem]).start()

    def take(ref, sem):
        pltpu.make_async_copy(ref, ref, sem).wait()

    def remote(src, dst, send, recv, to):
        return pltpu.make_async_remote_copy(
            src_ref=src, dst_ref=dst, send_sem=send, recv_sem=recv,
            device_id=to, device_id_type=MESH)

    def slot(direction, d):
        return {0: 0, 4: 1}.get(d, 2 * d + direction)

    def z_copy(h, part, direction, d):
        src = kv.at[h, slot(direction, d - 1), core]
        dst = kv.at[h, slot(direction, d), core]
        if part is not None:
            src, dst = src.at[part], dst.at[part]
        if d == 1:
            src = (vk, vv)[part].at[:, pl.ds(h * HEAD_DIM, HEAD_DIM)]
        return remote(src, dst, send_sem.at[0], z_recv.at[h, direction, d - 1],
                      up if direction == 0 else down)

    def s_copy(h, place, step):
        ref = kv.at[h, place, core]
        return remote(ref, ref, send_sem.at[1], s_recv.at[h, step], sibling)

    def s_own(h, part):
        return remote((vk, vv)[part].at[:, pl.ds(h * HEAD_DIM, HEAD_DIM)], kv.at[h, 0, core, part],
                      send_sem.at[1], s_recv.at[h, 0], sibling)

    def q_copy(k):
        return remote(vq, q.at[pl.ds(GROUP[NX - k], ROWS)], send_sem.at[2], once_recv.at[0],
                      x_device(k))

    pl.semaphore_wait(barrier, len(peers))
    for h in range(HEADS):
        for direction in range(2):
            z_copy(h, 0, direction, 1).start()
            z_copy(h, 1, direction, 1).start()
    for k in (2, 1, 3):
        q_copy(k).start()
    for h in range(HEADS):
        for part in range(2):
            s_own(h, part).start()
    load(mask, reach, 0)
    for h in range(HEADS):
        for part, ref in enumerate((vk, vv)):
            load(ref.at[:, pl.ds(h * HEAD_DIM, HEAD_DIM)], kv.at[h, 0, core, part], 1)
    load(vq, q.at[pl.ds(GROUP[0], ROWS)], 2)
    load(tq.at[pl.ds(row_id * TXT_ROWS, TXT_ROWS)], q.at[pl.ds(TEXT, TXT_ROWS)], 3)
    far_id = (row_id + NZ) % (2 * NZ)
    load(tq.at[pl.ds(far_id * TXT_ROWS, TXT_ROWS)], q.at[pl.ds(FAR, TXT_ROWS)], 6)
    for part, ref in enumerate((tk, tv)):
        load(ref.at[pl.ds(x * TXT_KEYS, TXT_KEYS)], tkv.at[part, pl.ds(0, TXT_KEYS)], 4)
    signal(up_sem.at[0], y_device(1))
    signal(down_sem.at[0], y_device(NY - 1))
    signal(up_sem.at[3], up)
    signal(down_sem.at[3], down)
    for k in range(NY):
        load(w.at[:, pl.ds(((y + k) % NY) * FEATURES, FEATURES)], wbuf.at[k], 5)
    take(reach, load_sem.at[0])

    for s in range(5):
        for half in range(2):
            cols = slice(half * HEAD_DIM, (half + 1) * HEAD_DIM)
            if half == 1 and s == 4:
                continue
            if half == 1 and s == 0:
                lane = lax.broadcasted_iota(jnp.int32, (QUERIES, HEAD_DIM), 1)
                row = lax.broadcasted_iota(jnp.int32, (QUERIES, HEAD_DIM), 0)
                bias[0, :, cols] = jnp.where((lane < TXT_KEYS) & (row < FAR), 0.0, NEG).astype(F32)
                continue
            tile_z = (z + NZ - s) % NZ if half == 0 else (z + s) % NZ
            for k in range(NX):
                if GROUP[k] >= USED[s]:
                    continue
                allowed = reach[z * NX + (x + k) % NX, tile_z * NX + x].astype(F32)
                bias[s, GROUP[k]:GROUP[k] + ROWS, cols] = jnp.full(
                    (ROWS, HEAD_DIM), (1.0 - allowed) * NEG, F32)
            for first in (TEXT, FAR):
                if first < USED[s]:
                    bias[s, first:first + TXT_ROWS, cols] = jnp.zeros((TXT_ROWS, HEAD_DIM), F32)
    for part in range(2):
        tkv[part, TXT_KEYS:] = jnp.zeros((HEAD_DIM - TXT_KEYS, FEATURES), BF16)

    def pass_on(sem):
        pl.semaphore_wait(up_sem.at[sem - 1], 1)
        pl.semaphore_wait(down_sem.at[sem - 1], 1)
        signal(up_sem.at[sem], up)
        signal(down_sem.at[sem], down)

    pass_on(4)
    ones = jnp.ones((STEP_KEYS, HEAD_DIM), BF16)

    def absorb(h, s):
        cols = slice(h * HEAD_DIM, (h + 1) * HEAD_DIM)
        slots = {0: (0,), 4: (1,)}.get(s, (2 * s, 2 * s + 1))
        used = USED[s]
        keys = [kv[h, slot, cc, 0] for slot in slots for cc in range(2)]
        values = [kv[h, slot, cc, 1] for slot in slots for cc in range(2)]
        if s == 0:
            keys.append(tkv[0, :, cols])
            values.append(tkv[1, :, cols])
        keys, values = jnp.concatenate(keys, 0), jnp.concatenate(values, 0)
        count = keys.shape[0]
        scores = lax.dot_general(q[:used, cols], keys, (((1,), (1,)), ((), ())),
                                 preferred_element_type=F32)
        scores = scores * SCALE + bias[s, :used, :count]
        high = jnp.max(scores, axis=1, keepdims=True)
        if s:
            before = top[h, :used][:, :1]
            high = jnp.maximum(high, before)
        weights = jnp.exp2(scores - high).astype(BF16)
        values = jnp.concatenate([values, ones[:count]], 1)
        summed = jnp.dot(weights, values, preferred_element_type=F32)
        if s:
            summed = summed + acc[h, :used] * jnp.exp2(before - high)
        if s == 4:
            return summed[:, :HEAD_DIM] / summed[:, HEAD_DIM:]
        acc[h, :used] = summed
        top[h, :used] = jnp.broadcast_to(high, (used, HEAD_DIM))

    def forward(h, d):
        for direction in range(2):
            if d < 4:
                ref = kv.at[h, slot(direction, d), core]
            else:
                ref = kv.at[h, 1, core, direction]
            take(ref, z_recv.at[h, direction, d - 1])
            if d < 4:
                z_copy(h, direction if d == 3 else None, direction, d + 1).start()
        for place in (slot(0, d), slot(1, d)) if d < 4 else (1,):
            s_copy(h, place, d).start()

    def from_sibling(h, s):
        places = {0: 0, 4: 1}.get(s, pl.ds(2 * s, 2))
        take(kv.at[h, places, 1 - core], s_recv.at[h, s])

    def eye(rows):
        return (lax.broadcasted_iota(jnp.int32, (rows, HEAD_DIM), 0)
                == lax.broadcasted_iota(jnp.int32, (rows, HEAD_DIM), 1))

    def finish(h, first, rows):
        block = slice(first, first + rows)
        total = acc[h, block, HEAD_DIM:]
        return acc[h, block, :HEAD_DIM] / total, top[h, block] + jnp.log2(total)

    def to_rows(level):
        row = jnp.sum(jnp.where(eye(level.shape[0]), level, 0.0), axis=0, keepdims=True)
        first = row.astype(BF16).astype(F32)
        second = (row - first).astype(BF16).astype(F32)
        index = lax.broadcasted_iota(jnp.int32, (16, HEAD_DIM), 0)
        rest = jnp.where(index == 1, second, jnp.where(index == 2, row - first - second, 0.0))
        return jnp.where(index == 0, first, rest).astype(BF16)

    def to_column(rows, count):
        row = rows[0:1] + rows[1:2] + rows[2:3]
        return jnp.sum(jnp.where(eye(count), jnp.broadcast_to(row, (count, HEAD_DIM)), 0.0),
                       axis=1, keepdims=True)

    def o_copy(h, k):
        return remote(osend.at[h, k - 1], orecv.at[h, k - 1], send_sem.at[3], o_recv.at[h, k - 1],
                      x_device(k))

    def give(h, k):
        block, level = finish(h, GROUP[k], ROWS)
        osend[h, k - 1, :ROWS] = block.astype(BF16)
        osend[h, k - 1, ROWS:] = to_rows(level)
        o_copy(h, k).start()

    def fold(h, first, rows, sources):
        block = slice(first, first + rows)
        before = top[h, block][:, :1]
        parts, levels = [acc[h, block]], [before]
        for source in sources:
            part = source[:rows].astype(F32)
            parts.append(jnp.concatenate([part, jnp.ones((rows, HEAD_DIM), F32)], 1))
            levels.append(to_column(source[rows:].astype(F32), rows))
        high = functools.reduce(jnp.maximum, levels)
        acc[h, block] = functools.reduce(
            jnp.add, [part * jnp.exp2(level - high) for part, level in zip(parts, levels)])
        top[h, block] = jnp.broadcast_to(high, (rows, HEAD_DIM))

    def pack_text(h, first, to):
        part, level = finish(h, first, TXT_ROWS)
        to[h, :TXT_ROWS] = part.astype(BF16)
        to[h, TXT_ROWS:] = to_rows(level)

    def merge(parts, levels):
        high = functools.reduce(jnp.maximum, levels)
        shares = [jnp.exp2(level - high) for level in levels]
        total = functools.reduce(jnp.add, shares)
        return functools.reduce(
            jnp.add, [part * (share / total) for part, share in zip(parts, shares)]).astype(BF16)

    for h in range(HEADS):
        forward(h, 1)
    pass_on(5)
    take(kv.at[:, 0, core], load_sem.at[1])
    take(q.at[pl.ds(GROUP[0], ROWS)], load_sem.at[2])
    take(q.at[pl.ds(TEXT, TXT_ROWS)], load_sem.at[3])
    take(q.at[pl.ds(FAR, TXT_ROWS)], load_sem.at[6])
    take(tkv.at[:, pl.ds(0, TXT_KEYS)], load_sem.at[4])
    take(q.at[pl.ds(GROUP[1], 3 * ROWS)], once_recv.at[0])
    for h in range(HEADS):
        from_sibling(h, 0)
        absorb(h, 0)
    for h in range(HEADS):
        pack_text(h, FAR, fsend)
    pl.semaphore_wait(up_sem.at[5], 1)
    pl.semaphore_wait(down_sem.at[5], 1)
    remote(fsend, frecv, send_sem.at[7], once_recv.at[6], device((z + 4) % NZ, x, core, y)).start()
    for h in range(HEADS):
        forward(h, 2)
        from_sibling(h, 1)
        absorb(h, 1)
        give(h, 2)
    pl.semaphore_wait(up_sem.at[0], 1)
    pl.semaphore_wait(down_sem.at[0], 1)
    signal(up_sem.at[1], y_device(1))
    signal(down_sem.at[1], y_device(NY - 1))
    for h in range(HEADS):
        forward(h, 3)
        from_sibling(h, 2)
        absorb(h, 2)
    pl.semaphore_wait(up_sem.at[1], 1)
    pl.semaphore_wait(down_sem.at[1], 1)
    signal(up_sem.at[2], y_device(1))
    signal(down_sem.at[2], y_device(NY - 1))
    for h in range(HEADS):
        from_sibling(h, 3)
        absorb(h, 3)
        give(h, 1)
        give(h, 3)

    def x_copy(k):
        return remote(tsend, trecv.at[k], send_sem.at[4], once_recv.at[1], x_device(k))

    take(frecv, once_recv.at[6])
    for h in range(HEADS):
        fold(h, TEXT, TXT_ROWS, [frecv.at[h]])
    for h in range(HEADS):
        pack_text(h, TEXT, tsend)
    for k in (2, 1, 3):
        x_copy(k).start()
    for h in range(HEADS):
        forward(h, 4)
    pl.semaphore_wait(up_sem.at[2], 1)
    pl.semaphore_wait(down_sem.at[2], 1)
    take(wbuf, load_sem.at[5])

    for h in range(HEADS):
        for k in range(1, NX):
            o_copy(h, k).wait_recv()
    for h in range(HEADS):
        fold(h, GROUP[0], ROWS, [orecv.at[h, k - 1] for k in range(1, NX)])
    for h in range(HEADS):
        from_sibling(h, 4)
    for h in range(HEADS):
        attn[:, h * HEAD_DIM:(h + 1) * HEAD_DIM] = absorb(h, 4).astype(BF16)

    def product(k):
        return jnp.dot(attn[...], wbuf[k], preferred_element_type=F32)

    halves = (slice(0, ROWS // 2), slice(ROWS // 2, ROWS))

    def y_copy(k, half=None, way=0):
        to = {3: 1, 5: NY - 1, 4: (2, NY - 2)[way]}.get(k, k)
        src, dst, sem = ysend.at[PLACE[k]], yrecv.at[PLACE[k]], once_recv.at[4]
        if half is not None:
            rows = pl.ds(half * (ROWS // 2), ROWS // 2)
            src, dst = src.at[rows], dst.at[rows]
        if k in (3, 4, 5):
            sem = relay_recv.at[PLACE[k], half]
        return remote(src, dst, send_sem.at[5], sem, y_device(to))

    ysend[PLACE[4]] = product(4).astype(BF16)
    for half in range(2):
        y_copy(4, half, half).start()
    for k in (3, 5):
        ysend[PLACE[k]] = product(k).astype(BF16)
    for first in range(2):
        y_copy(3, 1 - first).start()
        y_copy(5, first).start()

    mine = tout.at[row_id]
    take(trecv.at[pl.ds(1, NX - 1)], once_recv.at[1])
    trecv[0] = tsend[...]
    for h in range(HEADS):
        parts = [trecv[k, h, :TXT_ROWS].astype(F32) for k in range(NX)]
        levels = [to_column(trecv[k, h, TXT_ROWS:].astype(F32), TXT_ROWS) for k in range(NX)]
        mine[:, h * HEAD_DIM:(h + 1) * HEAD_DIM] = merge(parts, levels)
    for k in (8, 9, 7, 10, 6, 11, 5, 12, 4, 13, 3, 14, 2, 15, 1):
        other = (row_id + k) % (2 * NZ)
        to = device(other // 2, x, other % 2, y)
        remote(mine, mine, send_sem.at[6], once_recv.at[5], to).start()

    for way, k in enumerate((2, 6)):
        yterm[way] = product(k)
    for step in range(2):
        for way, (k, relay) in enumerate(((2, 3), (6, 5))):
            half = way if step else 1 - way
            rows = halves[half]
            y_copy(relay, half).wait_recv()
            yterm[way, rows] += yrecv[PLACE[relay], rows].astype(F32)
            if step:
                y_copy(4, half, way).wait_recv()
                yterm[way, rows] += yrecv[PLACE[4], rows].astype(F32)
            ysend[PLACE[k], rows] = yterm[way, rows].astype(BF16)
            y_copy(k, half).start()
    for k in (1, 7):
        ysend[PLACE[k]] = product(k).astype(BF16)
        y_copy(k).start()
    total = product(0)

    take(yrecv.at[pl.ds(3, 4)], once_recv.at[4])
    for k in (1, 2, 6, 7):
        total = total + yrecv[PLACE[k]].astype(F32)
    out[...] = total.astype(BF16)

    others = tout.at[pl.ds(0, 2 * NZ - 1)]
    take(others, once_recv.at[5])
    for index, ref in enumerate((kv.at[:, pl.ds(0, 7), 0], kv.at[:, :, 0],
                                 q.at[pl.ds(GROUP[1], 3 * ROWS)], osend,
                                 trecv.at[pl.ds(1, NX - 1)], ysend, others, fsend)):
        take(ref, send_sem.at[index])


def local(video_q, video_k, video_v, text_q, text_k, text_v, tile_mask, out_weight):
    hbm = pl.BlockSpec(memory_space=pltpu.HBM)
    vmem = pl.BlockSpec(memory_space=pltpu.VMEM)
    dma = pltpu.SemaphoreType.DMA
    in_hbm = functools.partial(pltpu.with_memory_space_constraint, memory_space=pltpu.HBM)
    regular = pltpu.SemaphoreType.REGULAR
    video, text = pl.pallas_call(
        body,
        out_shape=(
            jax.ShapeDtypeStruct((ROWS, FEATURES), BF16),
            jax.ShapeDtypeStruct((2 * NZ, TXT_ROWS, FEATURES), BF16),
        ),
        in_specs=[hbm] * 6 + [hbm, hbm],
        out_specs=(vmem, vmem),
        scratch_shapes=[
            pltpu.VMEM((QUERIES, FEATURES), BF16),
            pltpu.VMEM((HEADS, NZ, 2, 2, ROWS, HEAD_DIM), BF16),
            pltpu.VMEM((2, HEAD_DIM, FEATURES), BF16),
            pltpu.VMEM((5, QUERIES, STEP_KEYS), F32),
            pltpu.VMEM((HEADS, QUERIES, 2 * HEAD_DIM), F32),
            pltpu.VMEM((HEADS, QUERIES, HEAD_DIM), F32),
            pltpu.VMEM((HEADS, NX - 1, ROWS + 16, HEAD_DIM), BF16),
            pltpu.VMEM((HEADS, NX - 1, ROWS + 16, HEAD_DIM), BF16),
            pltpu.VMEM((HEADS, TXT_ROWS + 16, HEAD_DIM), BF16),
            pltpu.VMEM((NX, HEADS, TXT_ROWS + 16, HEAD_DIM), BF16),
            pltpu.VMEM((HEADS, TXT_ROWS + 16, HEAD_DIM), BF16),
            pltpu.VMEM((HEADS, TXT_ROWS + 16, HEAD_DIM), BF16),
            pltpu.VMEM((ROWS, FEATURES), BF16),
            pltpu.VMEM((NY, FEATURES, FEATURES), BF16),
            pltpu.VMEM((NY - 1, ROWS, FEATURES), BF16),
            pltpu.VMEM((NY - 1, ROWS, FEATURES), BF16),
            pltpu.VMEM((2, ROWS, FEATURES), F32),
            pltpu.SMEM((TILES, TILES), jnp.int32),
            dma((7,)),
            dma((8,)),
            dma((HEADS, 2, 4)),
            dma((HEADS, 5)),
            dma((HEADS, NX - 1)),
            dma((7,)),
            dma((3, 2)),
            regular((6,)), regular((6,)),
        ],
        compiler_params=pltpu.CompilerParams(
            collective_id=0, has_side_effects=True, vmem_limit_bytes=40 * 2**20),
    )(*map(in_hbm, (video_q, video_k, video_v, text_q, text_k, text_v, tile_mask, out_weight)))
    return video, text.reshape(2 * NZ * TXT_ROWS, FEATURES)


def solution(mesh):
    placed = (
        P("ctx", "head"),
        P("ctx", "head"),
        P("ctx", "head"),
        P(None, "head"),
        P(None, "head"),
        P(None, "head"),
        P(),
        P("head", None),
    )
    return jax.shard_map(
        local,
        mesh=mesh,
        in_specs=placed,
        out_specs=(P("ctx", "head"), P(None, "head")),
        check_vma=False,
    )
```
